512 devices in a mesh: season: 8 (over y), row: 8 (over z_lo, x), col: 8 (over z_hi, core).
Axes of the slice: x: 4, y: 8, z: 8 (z_hi: 4, z_lo: 2; z = z_hi * 2 + z_lo), core: 2. Of those that a mesh axis runs over, the one named last changes fastest.
Arguments:
- tiles: float32 [8, 8, 8, 32, 128, 128], P('season', 'row', 'col'), may hold values from -0.125 to 0.125
- tile_rows: int32 [8, 8, 8, 32], P('season', 'row', 'col'), may hold values from 0 to 15, as said below
- tile_cols: int32 [8, 8, 8, 32], P('season', 'row', 'col'), may hold values from 0 to 15, as said below
- rhs: float32 [8, 16384], P('season', 'row')
- coupling: float32 [8, 16384], P('season', 'row'), may hold values from -1 to -0.2
- asset: int32 [8, 16384], P('season', 'row'), may hold values from 0 to 65535
- cost_x: float32 [8, 16384], P('season', 'col'), may hold values from -6 to 6
- upper: float32 [8, 16384], P('season', 'col'), may hold values from 0.5 to 4
- cost_z: float32 [65536], replicated, may hold values from 0.2 to 2
- x_init: float32 [8, 16384], P('season', 'col'), may hold values from 0 to 1
- z_init: float32 [65536], replicated, may hold values from 0 to 1
- y_init: float32 [8, 16384], P('season', 'row'), may hold values from 0 to 1
Outputs:
- x_final: float32 [8, 16384], P('season', 'col')
- z_final: float32 [65536], replicated
- y_final: float32 [8, 16384], P('season', 'row')
The draws below stay inside these ranges and needn't reach their ends.
Inputs may be any that keep to these rules, and one draw needn't show every extreme that they name: `tile_rows`: within each device's part, the tiles sit at distinct positions, and every block row and every block column holds exactly two tiles. `tile_cols`: see tile_rows: every block column of a device's part holds exactly two tiles.
All inputs are finite; a program needn't handle non-finite values.
Results may differ from the reference program's by a relative error of at most 0.0003.
Values sent between devices are 32-bit elements; how exact they have to be, the bound alone decides.
A program may use at most 64 MiB of HBM per device.

```python
import math
import jax
import jax.numpy as jnp
from jax import lax

NB = 16
TILE = 128
NINV = 65536
ITERS = 3
TILES = 32
SEASONS = 8
ROWBLK = 8
COLBLK = 8
NROWS = 16384
NCOLS = 16384
N_COL = 8


def tile_pattern(key):
    prefix = (SEASONS, ROWBLK, COLBLK)
    row_scores = jax.random.randint(jax.random.fold_in(key, 11), prefix + (NB,), 0, 2 ** 30)
    col_scores = jax.random.randint(jax.random.fold_in(key, 12), prefix + (NB,), 0, 2 ** 30)
    row_perm = jnp.argsort(row_scores, axis=-1, stable=True).astype(jnp.int32)
    col_perm = jnp.argsort(col_scores, axis=-1, stable=True).astype(jnp.int32)
    shifts = jax.random.randint(jax.random.fold_in(key, 13), prefix + (1,), 1, NB)
    moved = (jnp.arange(NB, dtype=jnp.int32)[None, None, None, :] + shifts) % NB
    second = jnp.take_along_axis(col_perm, moved.astype(jnp.int32), axis=-1)
    rows_out = jnp.concatenate([row_perm, row_perm], axis=-1)
    cols_out = jnp.concatenate([col_perm, second], axis=-1)
    return (rows_out.astype(jnp.int32), cols_out.astype(jnp.int32))


def draw_tile_rows(key, part):
    return tile_pattern(key)[0]


def draw_tile_cols(key, part):
    return tile_pattern(key)[1]


def draw_rhs(key, part):
    key = jax.random.fold_in(key, 3)
    season_scale = 1.0 + 2.0 * jnp.arange(SEASONS, dtype=jnp.float32) / max(SEASONS - 1, 1)
    row_scale = 1.0 + 2.0 * jnp.arange(NROWS, dtype=jnp.float32) / (NROWS - 1)
    base = jax.random.normal(key, (SEASONS, NROWS), jnp.float32)
    return (base * season_scale[:, None] * row_scale[None, :]).astype(jnp.float32)


def touch_ends(result, stream_key, low, top_value):
    longest = result.shape.index(max(result.shape))
    spots = []
    for shift in (0, 1):
        where = [jax.random.randint(jax.random.fold_in(stream_key, axis), (), 0, length) for axis, length in enumerate(result.shape)]
        where[longest] = (where[longest] + shift) % result.shape[longest]
        spots.append(tuple(where))
    return result.at[spots[0]].set(low).at[spots[1]].set(top_value)


def shard_levels(stream_key, extent, shards, low, largest):
    factor_of, own = 1.0, jax.random.fold_in(stream_key, 6)
    for axis_at, blocks in shards:
        steps = jnp.exp(jax.random.uniform(jax.random.fold_in(own, axis_at), (blocks,), jnp.float32, low / len(shards), largest / len(shards)))
        factor_of = factor_of * jnp.repeat(steps, extent[axis_at] // blocks).reshape([-1 if axis == axis_at else 1 for axis in range(len(extent))])
    return factor_of


def scatter_about(own_key, dims, deviation, most, pieces=(), kind=jnp.bfloat16):
    result = jax.random.normal(own_key, dims, jnp.float32) * deviation
    if len(pieces) > 0:
        result = shard_levels(own_key, dims, pieces, -0.22, 0.18) * result
    return jnp.clip(result, min=-most, max=most).astype(kind)


def setup_inputs(seed: int = 0) -> dict:
    seeds = jax.random.split(jax.random.key(seed), 13)
    return {
        "tiles": scatter_about(seeds[0], (SEASONS, ROWBLK, COLBLK, TILES, TILE, TILE), (2 * N_COL * TILE) ** -0.5, 0.125, ((0, 8), (1, 8), (2, 8)), jnp.float32),
        "tile_rows": draw_tile_rows(jax.random.fold_in(seeds[12], 71), 0),
        "tile_cols": draw_tile_cols(jax.random.fold_in(seeds[12], 71), 0),
        "rhs": draw_rhs(jax.random.fold_in(seeds[12], 71), 0),
        "coupling": jnp.clip(-1.0 + 0.8 * jax.random.uniform(seeds[4], (SEASONS, NROWS), jnp.float32) ** shard_levels(seeds[4], (SEASONS, NROWS), ((0, 8), (1, 8)), -0.2, 0.2), -1.0, -0.2),
        "asset": touch_ends(jax.random.randint(seeds[5], (SEASONS, NROWS), 0, NINV), jax.random.fold_in(seeds[5], 1), 0, NINV - 1).astype(jnp.int32),
        "cost_x": scatter_about(seeds[6], (SEASONS, NCOLS), 1.0, 6.0, ((0, 8), (1, 8)), jnp.float32),
        "upper": jnp.clip(jnp.exp(math.log(4.0) - 2.0794415 * jax.random.uniform(seeds[7], (SEASONS, NCOLS), jnp.float32) ** shard_levels(seeds[7], (SEASONS, NCOLS), ((0, 8), (1, 8)), -0.2, 0.2)), 0.5, 4.0),
        "cost_z": jnp.clip(jnp.exp(jax.random.uniform(seeds[8], (NINV,), jnp.float32, math.log(0.2), math.log(2.0))), 0.2, 2.0),
        "x_init": jnp.clip(1.0 * jax.random.uniform(seeds[9], (SEASONS, NCOLS), jnp.float32) ** shard_levels(seeds[9], (SEASONS, NCOLS), ((0, 8), (1, 8)), -0.2, 0.2), 0.0, 1.0),
        "z_init": jnp.clip(jax.random.uniform(seeds[10], (NINV,), jnp.float32, 0.0, 1.0), 0.0, 1.0),
        "y_init": jnp.clip(1.0 * jax.random.uniform(seeds[11], (SEASONS, NROWS), jnp.float32) ** shard_levels(seeds[11], (SEASONS, NROWS), ((0, 8), (1, 8)), -0.2, 0.2), 0.0, 1.0),
    }


STEP_SCALE = 0.35
EPSILON = 1e-06

def forward_group(tile_vals, tile_rows, tile_cols, values):
    blocks = values.reshape(COLBLK, NB, TILE)
    picked = blocks[jnp.arange(COLBLK)[None, :, None], tile_cols]
    product = jnp.einsum('rcktu,rcku->rckt', tile_vals, picked, precision=lax.Precision.HIGHEST)
    landing = (tile_rows[..., None] == jnp.arange(NB)).astype(jnp.float32)
    return jnp.einsum('rckt,rckn->rnt', product, landing, precision=lax.Precision.HIGHEST).reshape(-1)

def backward_group(tile_vals, tile_rows, tile_cols, values):
    blocks = values.reshape(ROWBLK, NB, TILE)
    picked = blocks[jnp.arange(ROWBLK)[:, None, None], tile_rows]
    product = jnp.einsum('rcktu,rckt->rcku', tile_vals, picked, precision=lax.Precision.HIGHEST)
    landing = (tile_cols[..., None] == jnp.arange(NB)).astype(jnp.float32)
    return jnp.einsum('rcku,rckn->cnu', product, landing, precision=lax.Precision.HIGHEST).reshape(-1)

def reference(tiles, tile_rows, tile_cols, rhs, coupling, asset, cost_x, upper, cost_z, x_init, z_init, y_init):
    primal, invest, duals = (x_init, z_init, y_init)
    balance = jnp.float32(1.0)
    for iteration in range(ITERS):
        primal_step = STEP_SCALE / balance
        dual_step = STEP_SCALE * balance
        transposed = lax.map(lambda item: backward_group(*item), (tiles, tile_rows, tile_cols, duals))
        capacity = jax.ops.segment_sum((coupling * duals).reshape(-1), asset.reshape(-1), num_segments=NINV)
        new_x = jnp.clip(primal - primal_step * (cost_x - transposed), 0.0, upper)
        new_z = jnp.maximum(invest - primal_step * (cost_z - capacity), 0.0)
        extra_x = 2.0 * new_x - primal
        extra_z = 2.0 * new_z - invest
        image = lax.map(lambda item: forward_group(*item), (tiles, tile_rows, tile_cols, extra_x))
        image = image + coupling * extra_z[asset]
        new_y = jnp.maximum(duals + dual_step * (rhs - image), 0.0)
        if iteration + 1 < ITERS:
            primal_sq = jnp.sum((new_x - primal) ** 2) + jnp.sum((new_z - invest) ** 2)
            dual_sq = jnp.sum((new_y - duals) ** 2)
            balance = jnp.sqrt(balance * jnp.sqrt((primal_sq + EPSILON) / (dual_sq + EPSILON)))
        primal, invest, duals = (new_x, new_z, new_y)
    return (primal, invest, duals)
```

```python
import functools

import jax
import jax.numpy as jnp
from jax import lax
from jax.experimental import pallas as pl
from jax.experimental.pallas import tpu as pltpu
from jax.sharding import PartitionSpec as P

ITERS = 3
STEP_SCALE = 0.35
EPSILON = 1e-06

MESH = pl.DeviceIdType.MESH
F32, BF16, I32 = jnp.float32, jnp.bfloat16, jnp.int32
G = 8
NB = 16
TILE = 128
TILES = 32
CH = 64
SUB = CH // G


def peer(axis, k):
    return {axis: lax.rem(lax.axis_index(axis) + k, G)}


def to_peers(axis, copy):
    for k in range(1, G):
        copy(lax.rem(lax.axis_index(axis) + k, G), peer(axis, k))


def wait_bytes(ref, sem):
    pltpu.make_async_copy(ref, ref, sem).wait()


def split2(v):
    high = v.astype(BF16)
    return high, (v - high.astype(F32)).astype(BF16)


def first_and_last(keys, other):
    k = lax.broadcasted_iota(I32, (NB, TILES), 1)
    hit = keys == lax.broadcasted_iota(I32, (NB, TILES), 0)
    one = jnp.min(jnp.where(hit, k, TILES - 1), axis=1, keepdims=True)
    two = jnp.max(jnp.where(hit, k, 0), axis=1, keepdims=True)
    pick = lambda t: jnp.sum(jnp.where(k == t, other, 0), axis=1, keepdims=True)
    return one, two, pick(one), pick(two)


def products(order, column, tiles_ref, values_ref, picked, out):
    for b in range(NB):
        picked[b : b + 1, 0:TILE] = values_ref[pl.ds(order[b, column + 2], 1), :]
        picked[b : b + 1, TILE : 2 * TILE] = values_ref[pl.ds(order[b, column + 3], 1), :]
    high, low = split2(picked[...])
    left = jnp.concatenate([high, low], axis=0)
    for b in range(NB):
        right = jnp.concatenate(
            [tiles_ref[order[b, column]], tiles_ref[order[b, column + 1]]], axis=0
        )
        res = jnp.dot(left, right, preferred_element_type=F32)
        row = res[b : b + 1, :] + res[NB + b : NB + b + 1, :]
        out(b, row[:, 0:TILE] + row[:, TILE : 2 * TILE])


def kernel(
    tiles_hbm, rows_ref, cols_ref, rhs_ref, coup_ref, asset_ref, costx_ref, upper_ref, costz_hbm, x0_ref, z0_hbm, y0_ref,
    x_out, z_out, y_out,
    tiles, tb, tf, costz, zv, xv, yv, tr, fw, picked, order_v, order, hot_hi, hot_lo, left,
    gsend, rs, rx, sx, ez, cx, zall,
    load_sem, order_sem, send_sem, recv_sem, zs_sem, zr_sem,
):
    s, r, c = (lax.axis_index(a) for a in ("season", "row", "col"))
    barrier = pltpu.get_barrier_semaphore()
    for axis in ("season", "row", "col"):
        for k in range(1, G):
            pl.semaphore_signal(barrier, inc=1, device_id=peer(axis, k), device_id_type=MESH)
    mine = pl.ds(pl.multiple_of(c * CH + r * SUB, SUB), SUB)
    loads = [
        pltpu.make_async_copy(costz_hbm.at[mine], costz, load_sem.at[0]),
        pltpu.make_async_copy(z0_hbm.at[mine], zv, load_sem.at[1]),
        pltpu.make_async_copy(tiles_hbm, tiles, load_sem.at[2]),
    ]
    for load in loads:
        load.start()

    rows, cols = rows_ref[...], cols_ref[...]
    place = lax.broadcasted_iota(I32, (NB, TILE), 1)
    table = jnp.zeros((NB, TILE), I32)
    for at, col in enumerate(first_and_last(cols, rows) + first_and_last(rows, cols)):
        table = jnp.where(place == at, col, table)
    order_v[...] = table
    to_smem = pltpu.make_async_copy(order_v, order, order_sem)
    to_smem.start()

    asset = asset_ref[...]
    low, high = asset & (TILE - 1), (asset >> 7) - c * CH
    for n in range(NB):
        at = slice(n * TILE, (n + 1) * TILE)
        hit = lax.broadcasted_iota(I32, (TILE, TILE), 0) == low[n : n + 1, :]
        one = jnp.where(hit, 1.0, 0.0).astype(BF16)
        hot_lo[0:TILE, at] = one
        hot_lo[TILE : 2 * TILE, at] = one
        hit = lax.broadcasted_iota(I32, (CH, TILE), 0) == high[n : n + 1, :]
        hot_hi[:, at] = jnp.where(hit, 1.0, 0.0).astype(BF16)

    coup = coup_ref[...]
    xv[...] = x0_ref[...]
    yv[...] = y0_ref[...]
    balance = None
    stats = None
    for it in range(ITERS):
        last = it + 1 == ITERS
        srows = SUB if it == 0 else SUB + 2
        crows = NB if last else NB + 1
        sem = lambda phase: (send_sem.at[it, phase], recv_sem.at[it, phase])

        v_high, v_low = split2(coup * yv[...])
        for n in range(NB):
            at = slice(n * TILE, (n + 1) * TILE)
            hot = hot_hi[:, at]
            left[0:CH, at] = hot * v_high[n : n + 1, :]
            left[CH : 2 * CH, at] = hot * v_low[n : n + 1, :]
        cap = lax.dot_general(
            left[...], hot_lo[0:TILE, :], (((1,), (1,)), ((), ())), preferred_element_type=F32
        )
        cap = cap[0:CH] + cap[CH : 2 * CH]
        for k in range(G):
            gsend[it, k, 0:SUB] = cap[k * SUB : (k + 1) * SUB]
            if it:
                gsend[it, k, SUB : SUB + 2] = stats
        if it == 0:
            pl.semaphore_wait(barrier, 3 * (G - 1))
        sends, recvs = sem(0)

        def send(to, device):
            pltpu.make_async_remote_copy(
                src_ref=gsend.at[it, to, pl.ds(0, srows)], dst_ref=rs.at[it, r, pl.ds(0, srows)],
                send_sem=sends, recv_sem=recvs, device_id=device, device_id_type=MESH,
            ).start()

        to_peers("row", send)
        rs[it, r] = gsend[it, r]

        if it == 0:
            to_smem.wait()
            loads[2].wait()
            for k in range(TILES):
                t_high, t_low = split2(tiles[k])
                tb[k, :, 0:TILE] = t_high
                tb[k, :, TILE : 2 * TILE] = t_low

        def put(b, row):
            rx[it, r, b : b + 1, :] = row

        products(order, 0, tb, yv, picked, put)
        x_sends, x_recvs = sem(1)

        def send(to, device):
            pltpu.make_async_remote_copy(
                src_ref=rx.at[it, r], dst_ref=rx.at[it, r],
                send_sem=x_sends, recv_sem=x_recvs, device_id=device, device_id_type=MESH,
            ).start()

        to_peers("row", send)

        wait_bytes(rs.at[it, pl.ds(0, G - 1), pl.ds(0, srows)], recvs)
        sx[it, s, 0:srows] = jnp.sum(rs[it, :, 0:srows], axis=0)
        sends, recvs = sem(2)

        def send(to, device):
            pltpu.make_async_remote_copy(
                src_ref=sx.at[it, s, pl.ds(0, srows)], dst_ref=sx.at[it, s, pl.ds(0, srows)],
                send_sem=sends, recv_sem=recvs, device_id=device, device_id_type=MESH,
            ).start()

        to_peers("season", send)
        if it == 0:
            for k in range(TILES):
                t_high, t_low = split2(tiles[k].T)
                tf[k, :, 0:TILE] = t_high
                tf[k, :, TILE : 2 * TILE] = t_low
            loads[0].wait()
            loads[1].wait()
        wait_bytes(rx.at[it, pl.ds(0, G - 1)], x_recvs)
        transposed = jnp.sum(rx[it], axis=0)
        wait_bytes(sx.at[it, pl.ds(0, G - 1), pl.ds(0, srows)], recvs)
        total = jnp.sum(sx[it, :, 0:srows], axis=0)
        if it == 0:
            primal_step, dual_step = jnp.full((1, 1), STEP_SCALE, F32), jnp.full((1, 1), STEP_SCALE, F32)
        else:
            dual_sq = jnp.sum(total[SUB : SUB + 1], axis=1, keepdims=True)
            primal_sq = jnp.sum(total[SUB + 1 : SUB + 2], axis=1, keepdims=True) * (1.0 / G)
            root = jnp.sqrt((primal_sq + EPSILON) / (dual_sq + EPSILON))
            balance = jnp.sqrt(root if balance is None else balance * root)
            primal_step, dual_step = STEP_SCALE / balance, STEP_SCALE * balance

        z_old = zv[...]
        z_new = jnp.maximum(z_old - primal_step * (costz[...] - total[0:SUB]), 0.0)
        zv[...] = z_new
        ez[it, r] = 2.0 * z_new - z_old
        sends, recvs = sem(3)

        def send(to, device):
            pltpu.make_async_remote_copy(
                src_ref=ez.at[it, r], dst_ref=ez.at[it, r],
                send_sem=sends, recv_sem=recvs, device_id=device, device_id_type=MESH,
            ).start()

        to_peers("row", send)
        if last:
            zall[c, r] = z_new

            def send(to, device):
                pltpu.make_async_remote_copy(
                    src_ref=zall.at[c, r], dst_ref=zall.at[c, r],
                    send_sem=zs_sem.at[0], recv_sem=zr_sem.at[0], device_id=device, device_id_type=MESH,
                ).start()

            to_peers("row", send)

        x_old = xv[...]
        x_new = jnp.clip(x_old - primal_step * (costx_ref[...] - transposed), 0.0, upper_ref[...])
        xv[...] = x_new
        tr[...] = 2.0 * x_new - x_old

        def put(b, row):
            fw[b : b + 1, :] = row

        products(order, 4, tf, tr, picked, put)
        if last:
            x_out[...] = x_new
            wait_bytes(zall.at[0, pl.ds(0, G - 1)], zr_sem.at[0])
        else:
            cx[it, c, NB : NB + 1] = jnp.sum((x_new - x_old) ** 2, axis=0, keepdims=True) + jnp.sum(
                (z_new - z_old) ** 2, axis=0, keepdims=True
            )

        wait_bytes(ez.at[it, pl.ds(0, G - 1)], recvs)
        e_high, e_low = split2(ez[it].reshape(CH, TILE))
        gathered = jnp.dot(
            jnp.concatenate([e_high, e_low], axis=1), hot_lo[...], preferred_element_type=F32
        )
        for n in range(NB):
            at = slice(n * TILE, (n + 1) * TILE)
            linked = jnp.sum(gathered[:, at] * hot_hi[:, at].astype(F32), axis=0, keepdims=True)
            cx[it, c, n : n + 1] = fw[n : n + 1, :] + coup[n : n + 1, :] * linked
        sends, recvs = sem(4)

        def send(to, device):
            pltpu.make_async_remote_copy(
                src_ref=cx.at[it, c, pl.ds(0, crows)], dst_ref=cx.at[it, c, pl.ds(0, crows)],
                send_sem=sends, recv_sem=recvs, device_id=device, device_id_type=MESH,
            ).start()

        to_peers("col", send)
        if last:

            def send(to, device):
                pltpu.make_async_remote_copy(
                    src_ref=zall.at[c], dst_ref=zall.at[c],
                    send_sem=zs_sem.at[1], recv_sem=zr_sem.at[1], device_id=device, device_id_type=MESH,
                ).start()

            to_peers("col", send)
        wait_bytes(cx.at[it, pl.ds(0, G - 1), pl.ds(0, crows)], recvs)
        image = jnp.sum(cx[it, :, 0:crows], axis=0)

        y_old = yv[...]
        y_new = jnp.maximum(y_old + dual_step * (rhs_ref[...] - image[0:NB]), 0.0)
        yv[...] = y_new
        if last:
            y_out[...] = y_new
        else:
            stats = jnp.concatenate(
                [jnp.sum((y_new - y_old) ** 2, axis=0, keepdims=True), image[NB : NB + 1]], axis=0
            )

    wait_bytes(zall.at[pl.ds(0, G - 1)], zr_sem.at[1])
    z_out[...] = zall[...].reshape(G * CH, TILE)
    wait_bytes(zall.at[0, pl.ds(0, G - 1)], zs_sem.at[0])
    wait_bytes(zall.at[pl.ds(0, G - 1)], zs_sem.at[1])
    for it in range(ITERS):
        srows = SUB if it == 0 else SUB + 2
        crows = NB if it + 1 == ITERS else NB + 1
        wait_bytes(gsend.at[it, pl.ds(0, G - 1), pl.ds(0, srows)], send_sem.at[it, 0])
        wait_bytes(rx.at[it, pl.ds(0, G - 1)], send_sem.at[it, 1])
        wait_bytes(sx.at[it, pl.ds(0, G - 1), pl.ds(0, srows)], send_sem.at[it, 2])
        wait_bytes(ez.at[it, pl.ds(0, G - 1)], send_sem.at[it, 3])
        wait_bytes(cx.at[it, pl.ds(0, G - 1), pl.ds(0, crows)], send_sem.at[it, 4])


def local(
    tiles, tile_rows, tile_cols, rhs, coupling, asset, cost_x, upper, cost_z, x_init, z_init, y_init
):
    block = lambda a: a.reshape(NB, TILE)
    inside, anywhere = pl.BlockSpec(memory_space=pltpu.VMEM), pl.BlockSpec(memory_space=pl.ANY)
    x, z, y = pl.pallas_call(
        kernel,
        out_shape=(
            jax.ShapeDtypeStruct((NB, TILE), F32),
            jax.ShapeDtypeStruct((G * CH, TILE), F32),
            jax.ShapeDtypeStruct((NB, TILE), F32),
        ),
        in_specs=[anywhere] + [inside] * 7 + [anywhere, inside, anywhere, inside],
        out_specs=(inside, inside, inside),
        scratch_shapes=[
            pltpu.VMEM((TILES, TILE, TILE), F32),
            pltpu.VMEM((TILES, TILE, 2 * TILE), BF16),
            pltpu.VMEM((TILES, TILE, 2 * TILE), BF16),
            pltpu.VMEM((SUB, TILE), F32),
            pltpu.VMEM((SUB, TILE), F32),
            pltpu.VMEM((NB, TILE), F32),
            pltpu.VMEM((NB, TILE), F32),
            pltpu.VMEM((NB, TILE), F32),
            pltpu.VMEM((NB, TILE), F32),
            pltpu.VMEM((NB, 2 * TILE), F32),
            pltpu.VMEM((NB, TILE), I32),
            pltpu.SMEM((NB, TILE), I32),
            pltpu.VMEM((CH, NB * TILE), BF16),
            pltpu.VMEM((2 * TILE, NB * TILE), BF16),
            pltpu.VMEM((2 * CH, NB * TILE), BF16),
            pltpu.VMEM((ITERS, G, SUB + 2, TILE), F32),
            pltpu.VMEM((ITERS, G, SUB + 2, TILE), F32),
            pltpu.VMEM((ITERS, G, NB, TILE), F32),
            pltpu.VMEM((ITERS, G, SUB + 2, TILE), F32),
            pltpu.VMEM((ITERS, G, SUB, TILE), F32),
            pltpu.VMEM((ITERS, G, NB + 1, TILE), F32),
            pltpu.VMEM((G, G, SUB, TILE), F32),
            pltpu.SemaphoreType.DMA((3,)),
            pltpu.SemaphoreType.DMA,
            pltpu.SemaphoreType.DMA((ITERS, 5)),
            pltpu.SemaphoreType.DMA((ITERS, 5)),
            pltpu.SemaphoreType.DMA((2,)),
            pltpu.SemaphoreType.DMA((2,)),
        ],
        compiler_params=pltpu.CompilerParams(
            collective_id=0, has_side_effects=True, vmem_limit_bytes=32 * 1024 * 1024
        ),
    )(
        tiles.reshape(TILES, TILE, TILE),
        tile_rows.reshape(1, TILES),
        tile_cols.reshape(1, TILES),
        block(rhs),
        block(coupling),
        block(asset),
        block(cost_x),
        block(upper),
        cost_z.reshape(G * CH, TILE),
        block(x_init),
        z_init.reshape(G * CH, TILE),
        block(y_init),
    )
    return x.reshape(1, -1), z.reshape(-1), y.reshape(1, -1)


def solution(mesh):
    in_specs = (
        P("season", "row", "col", None, None, None),
        P("season", "row", "col", None),
        P("season", "row", "col", None),
        P("season", "row"),
        P("season", "row"),
        P("season", "row"),
        P("season", "col"),
        P("season", "col"),
        P(),
        P("season", "col"),
        P(),
        P("season", "row"),
    )
    out_specs = (P("season", "col"), P(), P("season", "row"))
    return jax.shard_map(local, mesh=mesh, in_specs=in_specs, out_specs=out_specs, check_vma=False)
```

```python
import functools

import jax
import jax.numpy as jnp
from jax import lax
from jax.experimental import pallas as pl
from jax.experimental.pallas import tpu as pltpu
from jax.sharding import PartitionSpec as P

ITERS = 3
STEP_SCALE = 0.35
EPSILON = 1e-06
VMEM_LIMIT = 32 * 1024 * 1024

MESH = pl.DeviceIdType.MESH
F32, BF16, I32 = jnp.float32, jnp.bfloat16, jnp.int32
G = 8
NB = 16
TILE = 128
TILES = 32
CH = 64
SUB = CH // G
HALF = pl.ds(0, SUB // 2), pl.ds(SUB // 2, SUB // 2)


NEAR = {"season": 8, "row": 4, "col": 2}
FAR_FIRST = {
    "season": [(0, 4), (0, 3), (0, 5), (0, 2), (0, 6), (0, 1), (0, 7)],
    "row": [(1, 2), (0, 2), (1, 1), (1, 3), (0, 1), (0, 3), (1, 0)],
    "col": [(2, 0), (2, 1), (1, 0), (3, 0), (1, 1), (3, 1), (0, 1)],
}


def others(axis):
    me, n = lax.axis_index(axis), NEAR[axis]
    i, j = me // n, lax.rem(me, n)
    return [lax.rem(i + a, G // n) * n + lax.rem(j + b, n) for a, b in FAR_FIRST[axis]]


def to_peers(axis, copy):
    for to in others(axis):
        copy(to, {axis: to})


def wait_bytes(ref, sem):
    pltpu.make_async_copy(ref, ref, sem).wait()


def split2(v):
    high = v.astype(BF16)
    return high, (v - high.astype(F32)).astype(BF16)


def first_and_last(keys, other):
    k = lax.broadcasted_iota(I32, (NB, TILES), 1)
    hit = keys == lax.broadcasted_iota(I32, (NB, TILES), 0)
    one = jnp.min(jnp.where(hit, k, TILES - 1), axis=1, keepdims=True)
    two = jnp.max(jnp.where(hit, k, 0), axis=1, keepdims=True)
    pick = lambda t: jnp.sum(jnp.where(k == t, other, 0), axis=1, keepdims=True)
    return one, two, pick(one), pick(two)


def products(order, column, tiles_ref, values_ref, picked, out):
    for b in range(NB):
        picked[b : b + 1, 0:TILE] = values_ref[pl.ds(order[b, column + 2], 1), :]
        picked[b : b + 1, TILE : 2 * TILE] = values_ref[pl.ds(order[b, column + 3], 1), :]
    high, low = split2(picked[...])
    left = jnp.concatenate([high, low], axis=0)
    for b in range(NB):
        right = jnp.concatenate(
            [tiles_ref[order[b, column]], tiles_ref[order[b, column + 1]]], axis=0
        )
        res = jnp.dot(left, right, preferred_element_type=F32)
        row = res[b : b + 1, :] + res[NB + b : NB + b + 1, :]
        out(b, row[:, 0:TILE] + row[:, TILE : 2 * TILE])


def kernel(
    tiles_hbm, rows_hbm, cols_hbm, rhs_hbm, coup_hbm, asset_hbm, costx_hbm, upper_hbm, costz_hbm, x0_hbm, z0_hbm, y0_hbm,
    x_out, z_out, y_out,
    tiles, rows_ref, cols_ref, rhs_ref, coup_ref, asset_ref, costx_ref, upper_ref, costz, xv, zv, yv,
    tb, tf, tr, fw, picked, order_v, order, mask, hot_hi, hot_lo, left,
    gsend, rs, rx, sx, ez, cx,
    load_sem, order_sem, send_sem, recv_sem, zs_sem, zr_sem,
):
    s, r, c = (lax.axis_index(a) for a in ("season", "row", "col"))
    barrier = pltpu.get_barrier_semaphore()
    for axis in ("season", "row", "col"):
        for to in others(axis):
            pl.semaphore_signal(barrier, inc=1, device_id={axis: to}, device_id_type=MESH)
    mine = pl.ds(pl.multiple_of(c * CH + r * SUB, SUB), SUB)
    loads = [
        pltpu.make_async_copy(there, here, load_sem.at[k])
        for k, (there, here) in enumerate([
            (asset_hbm, asset_ref), (coup_hbm, coup_ref), (y0_hbm, yv), (rows_hbm, rows_ref), (cols_hbm, cols_ref),
            (tiles_hbm, tiles), (costz_hbm.at[mine], costz), (z0_hbm.at[mine], zv), (x0_hbm, xv),
            (costx_hbm, costx_ref), (upper_hbm, upper_ref), (rhs_hbm, rhs_ref),
        ])
    ]
    for load in loads:
        load.start()

    loads[0].wait()
    asset = asset_ref[...]
    low, high = asset & (TILE - 1), (asset >> 7) - c * CH
    for n in range(NB):
        at = slice(n * TILE, (n + 1) * TILE)
        hit = lax.broadcasted_iota(I32, (TILE, TILE), 0) == low[n : n + 1, :]
        one = jnp.where(hit, 1.0, 0.0).astype(BF16)
        hot_lo[0:TILE, at] = one
        hot_lo[TILE : 2 * TILE, at] = one
        hit = lax.broadcasted_iota(I32, (CH, TILE), 0) == high[n : n + 1, :]
        one = jnp.where(hit, 1.0, 0.0)
        mask[:, at] = one
        hot_hi[:, at] = one.astype(BF16)

    loads[1].wait()
    loads[2].wait()
    coup = coup_ref[...]

    def send_z(k, axis, blocks):
        def send(to, device):
            pltpu.make_async_remote_copy(
                src_ref=blocks, dst_ref=blocks,
                send_sem=zs_sem.at[k], recv_sem=zr_sem.at[k], device_id=device, device_id_type=MESH,
            ).start()

        to_peers(axis, send)

    balance = None
    stats = None
    for it in range(ITERS):
        last = it + 1 == ITERS
        srows = SUB if it == 0 else SUB + 2
        crows = NB if last else NB + 1
        sem = lambda phase: (send_sem.at[it, phase], recv_sem.at[it, phase])

        v_high, v_low = split2(coup * yv[...])
        for n in range(NB):
            at = slice(n * TILE, (n + 1) * TILE)
            hot = hot_hi[:, at]
            left[0:CH, at] = hot * v_high[n : n + 1, :]
            left[CH : 2 * CH, at] = hot * v_low[n : n + 1, :]
        cap = lax.dot_general(
            left[...], hot_lo[0:TILE, :], (((1,), (1,)), ((), ())), preferred_element_type=F32
        )
        cap = cap[0:CH] + cap[CH : 2 * CH]
        for k in range(G):
            gsend[it, k, 0:SUB] = cap[k * SUB : (k + 1) * SUB]
            if it:
                gsend[it, k, SUB : SUB + 2] = stats
        if it == 0:
            pl.semaphore_wait(barrier, 3 * (G - 1))
        sends, recvs = sem(0)

        def send(to, device):
            pltpu.make_async_remote_copy(
                src_ref=gsend.at[it, to, pl.ds(0, srows)], dst_ref=rs.at[it, r, pl.ds(0, srows)],
                send_sem=sends, recv_sem=recvs, device_id=device, device_id_type=MESH,
            ).start()

        to_peers("row", send)
        rs[it, r] = gsend[it, r]

        if it == 0:
            loads[3].wait()
            loads[4].wait()
            rows, cols = rows_ref[...], cols_ref[...]
            place = lax.broadcasted_iota(I32, (NB, TILE), 1)
            table = jnp.zeros((NB, TILE), I32)
            for at, col in enumerate(first_and_last(cols, rows) + first_and_last(rows, cols)):
                table = jnp.where(place == at, col, table)
            order_v[...] = table
            to_smem = pltpu.make_async_copy(order_v, order, order_sem)
            to_smem.start()
            loads[5].wait()
            for k in range(TILES):
                t_high, t_low = split2(tiles[k])
                tb[k, :, 0:TILE] = t_high
                tb[k, :, TILE : 2 * TILE] = t_low
            to_smem.wait()

        def put(b, row):
            rx[it, r, b : b + 1, :] = row

        products(order, 0, tb, yv, picked, put)
        x_sends, x_recvs = sem(1)

        def send(to, device):
            pltpu.make_async_remote_copy(
                src_ref=rx.at[it, r], dst_ref=rx.at[it, r],
                send_sem=x_sends, recv_sem=x_recvs, device_id=device, device_id_type=MESH,
            ).start()

        to_peers("row", send)

        wait_bytes(rs.at[it, pl.ds(0, G - 1), pl.ds(0, srows)], recvs)
        sx[it, s, 0:srows] = jnp.sum(rs[it, :, 0:srows], axis=0)
        sends, recvs = sem(2)

        def send(to, device):
            pltpu.make_async_remote_copy(
                src_ref=sx.at[it, s, pl.ds(0, srows)], dst_ref=sx.at[it, s, pl.ds(0, srows)],
                send_sem=sends, recv_sem=recvs, device_id=device, device_id_type=MESH,
            ).start()

        to_peers("season", send)
        if it == 0:
            for k in range(TILES):
                t_high, t_low = split2(tiles[k].T)
                tf[k, :, 0:TILE] = t_high
                tf[k, :, TILE : 2 * TILE] = t_low
            for load in loads[6:]:
                load.wait()
        wait_bytes(rx.at[it, pl.ds(0, G - 1)], x_recvs)
        transposed = jnp.sum(rx[it], axis=0)
        wait_bytes(sx.at[it, pl.ds(0, G - 1), pl.ds(0, srows)], recvs)
        total = jnp.sum(sx[it, :, 0:srows], axis=0)
        if it == 0:
            primal_step, dual_step = jnp.full((1, 1), STEP_SCALE, F32), jnp.full((1, 1), STEP_SCALE, F32)
        else:
            dual_sq = jnp.sum(total[SUB : SUB + 1], axis=1, keepdims=True)
            primal_sq = jnp.sum(total[SUB + 1 : SUB + 2], axis=1, keepdims=True) * (1.0 / G)
            square = jnp.sqrt(primal_sq + EPSILON) * lax.rsqrt(dual_sq + EPSILON)
            if balance is not None:
                square = balance * square
            balance = jnp.sqrt(square)
            primal_step, dual_step = STEP_SCALE * lax.rsqrt(square), STEP_SCALE * balance

        z_old = zv[...]
        z_new = jnp.maximum(z_old - primal_step * (costz[...] - total[0:SUB]), 0.0)
        zv[...] = z_new
        ez[it, r] = 2.0 * z_new - z_old
        sends, recvs = sem(3)

        def send(to, device):
            pltpu.make_async_remote_copy(
                src_ref=ez.at[it, r], dst_ref=ez.at[it, r],
                send_sem=sends, recv_sem=recvs, device_id=device, device_id_type=MESH,
            ).start()

        to_peers("row", send)
        if last:
            z_out[c, r] = z_new
            send_z(0, "row", z_out.at[c, r, HALF[0]])
            send_z(2, "col", z_out.at[c, r, HALF[1]])

        x_old = xv[...]
        x_new = jnp.clip(x_old - primal_step * (costx_ref[...] - transposed), 0.0, upper_ref[...])
        xv[...] = x_new
        tr[...] = 2.0 * x_new - x_old

        def put(b, row):
            fw[b : b + 1, :] = row

        products(order, 4, tf, tr, picked, put)
        if last:
            x_out[...] = x_new
        else:
            cx[it, c, NB : NB + 1] = jnp.sum((x_new - x_old) ** 2, axis=0, keepdims=True) + jnp.sum(
                (z_new - z_old) ** 2, axis=0, keepdims=True
            )

        wait_bytes(ez.at[it, pl.ds(0, G - 1)], recvs)
        e_high, e_low = split2(ez[it].reshape(CH, TILE))
        gathered = jnp.dot(
            jnp.concatenate([e_high, e_low], axis=1), hot_lo[...], preferred_element_type=F32
        )
        for n in range(NB):
            at = slice(n * TILE, (n + 1) * TILE)
            linked = jnp.sum(gathered[:, at] * mask[:, at], axis=0, keepdims=True)
            cx[it, c, n : n + 1] = fw[n : n + 1, :] + coup[n : n + 1, :] * linked
        sends, recvs = sem(4)

        def send(to, device):
            pltpu.make_async_remote_copy(
                src_ref=cx.at[it, c, pl.ds(0, crows)], dst_ref=cx.at[it, c, pl.ds(0, crows)],
                send_sem=sends, recv_sem=recvs, device_id=device, device_id_type=MESH,
            ).start()

        to_peers("col", send)
        if last:
            wait_bytes(z_out.at[0, pl.ds(0, G - 1), HALF[0]], zr_sem.at[0])
            send_z(1, "col", z_out.at[c, :, HALF[0]])
            wait_bytes(z_out.at[pl.ds(0, G - 1), 0, HALF[1]], zr_sem.at[2])
            send_z(3, "row", z_out.at[:, r, HALF[1]])
        wait_bytes(cx.at[it, pl.ds(0, G - 1), pl.ds(0, crows)], recvs)
        image = jnp.sum(cx[it, :, 0:crows], axis=0)

        y_old = yv[...]
        y_new = jnp.maximum(y_old + dual_step * (rhs_ref[...] - image[0:NB]), 0.0)
        yv[...] = y_new
        if last:
            y_out[...] = y_new
        else:
            stats = jnp.concatenate(
                [jnp.sum((y_new - y_old) ** 2, axis=0, keepdims=True), image[NB : NB + 1]], axis=0
            )

    for half in range(2):
        step, blocks = HALF[half], pl.ds(0, G - 1)
        wait_bytes(z_out.at[blocks, :, step], zr_sem.at[2 * half + 1])
        wait_bytes(z_out.at[0, blocks, step], zs_sem.at[2 * half])
        wait_bytes(z_out.at[blocks, :, step], zs_sem.at[2 * half + 1])
    for it in range(ITERS):
        srows = SUB if it == 0 else SUB + 2
        crows = NB if it + 1 == ITERS else NB + 1
        wait_bytes(gsend.at[it, pl.ds(0, G - 1), pl.ds(0, srows)], send_sem.at[it, 0])
        wait_bytes(rx.at[it, pl.ds(0, G - 1)], send_sem.at[it, 1])
        wait_bytes(sx.at[it, pl.ds(0, G - 1), pl.ds(0, srows)], send_sem.at[it, 2])
        wait_bytes(ez.at[it, pl.ds(0, G - 1)], send_sem.at[it, 3])
        wait_bytes(cx.at[it, pl.ds(0, G - 1), pl.ds(0, crows)], send_sem.at[it, 4])


def place(x_ref, z_ref, y_ref, x_out, z_out, y_out, sem):
    copies = [
        pltpu.make_async_copy(here, there, sem.at[k])
        for k, (here, there) in enumerate([(z_ref, z_out), (x_ref, x_out), (y_ref, y_out)])
    ]
    for copy in copies:
        copy.start()
    for copy in copies:
        copy.wait()


def local(
    tiles, tile_rows, tile_cols, rhs, coupling, asset, cost_x, upper, cost_z, x_init, z_init, y_init
):
    block = lambda a: a.reshape(NB, TILE)
    inside = pl.BlockSpec(memory_space=pltpu.VMEM)
    in_hbm = lambda a: pltpu.with_memory_space_constraint(a, pltpu.HBM)
    in_vmem = lambda a: pltpu.with_memory_space_constraint(a, pltpu.VMEM)
    operands = (
        tiles.reshape(TILES, TILE, TILE),
        tile_rows.reshape(1, TILES),
        tile_cols.reshape(1, TILES),
        block(rhs),
        block(coupling),
        block(asset),
        block(cost_x),
        block(upper),
        cost_z.reshape(G * CH, TILE),
        block(x_init),
        z_init.reshape(G * CH, TILE),
        block(y_init),
    )
    x, z, y = pl.pallas_call(
        kernel,
        out_shape=(
            pltpu.VMEM((NB, TILE), F32), pltpu.VMEM((G, G, SUB, TILE), F32), pltpu.VMEM((NB, TILE), F32),
        ),
        in_specs=[pl.BlockSpec(memory_space=pltpu.HBM)] * 12,
        out_specs=(inside, inside, inside),
        scratch_shapes=[
            pltpu.VMEM((TILES, TILE, TILE), F32),
            pltpu.VMEM((1, TILES), I32),
            pltpu.VMEM((1, TILES), I32),
            pltpu.VMEM((NB, TILE), F32),
            pltpu.VMEM((NB, TILE), F32),
            pltpu.VMEM((NB, TILE), I32),
            pltpu.VMEM((NB, TILE), F32),
            pltpu.VMEM((NB, TILE), F32),
            pltpu.VMEM((SUB, TILE), F32),
            pltpu.VMEM((NB, TILE), F32),
            pltpu.VMEM((SUB, TILE), F32),
            pltpu.VMEM((NB, TILE), F32),
            pltpu.VMEM((TILES, TILE, 2 * TILE), BF16),
            pltpu.VMEM((TILES, TILE, 2 * TILE), BF16),
            pltpu.VMEM((NB, TILE), F32),
            pltpu.VMEM((NB, TILE), F32),
            pltpu.VMEM((NB, 2 * TILE), F32),
            pltpu.VMEM((NB, TILE), I32),
            pltpu.SMEM((NB, TILE), I32),
            pltpu.VMEM((CH, NB * TILE), F32),
            pltpu.VMEM((CH, NB * TILE), BF16),
            pltpu.VMEM((2 * TILE, NB * TILE), BF16),
            pltpu.VMEM((2 * CH, NB * TILE), BF16),
            pltpu.VMEM((ITERS, G, SUB + 2, TILE), F32),
            pltpu.VMEM((ITERS, G, SUB + 2, TILE), F32),
            pltpu.VMEM((ITERS, G, NB, TILE), F32),
            pltpu.VMEM((ITERS, G, SUB + 2, TILE), F32),
            pltpu.VMEM((ITERS, G, SUB, TILE), F32),
            pltpu.VMEM((ITERS, G, NB + 1, TILE), F32),
            pltpu.SemaphoreType.DMA((12,)),
            pltpu.SemaphoreType.DMA,
            pltpu.SemaphoreType.DMA((ITERS, 5)),
            pltpu.SemaphoreType.DMA((ITERS, 5)),
            pltpu.SemaphoreType.DMA((4,)),
            pltpu.SemaphoreType.DMA((4,)),
        ],
        compiler_params=pltpu.CompilerParams(
            collective_id=0, has_side_effects=True, vmem_limit_bytes=VMEM_LIMIT
        ),
    )(*map(in_hbm, operands))
    x, z, y = pl.pallas_call(
        place,
        out_shape=tuple(jax.ShapeDtypeStruct(a.shape, F32) for a in (x, z, y)),
        in_specs=[inside] * 3,
        out_specs=(pl.BlockSpec(memory_space=pl.ANY),) * 3,
        scratch_shapes=[pltpu.SemaphoreType.DMA((3,))],
    )(*map(in_vmem, (x, z, y)))
    return x.reshape(1, -1), z.reshape(-1), y.reshape(1, -1)


def solution(mesh):
    in_specs = (
        P("season", "row", "col", None, None, None),
        P("season", "row", "col", None),
        P("season", "row", "col", None),
        P("season", "row"),
        P("season", "row"),
        P("season", "row"),
        P("season", "col"),
        P("season", "col"),
        P(),
        P("season", "col"),
        P(),
        P("season", "row"),
    )
    out_specs = (P("season", "col"), P(), P("season", "row"))
    return jax.shard_map(local, mesh=mesh, in_specs=in_specs, out_specs=out_specs, check_vma=False)
```

```python
import functools

import jax
import jax.numpy as jnp
from jax import lax
from jax.experimental import pallas as pl
from jax.experimental.pallas import tpu as pltpu
from jax.sharding import PartitionSpec as P

ITERS = 3
STEP_SCALE = 0.35
EPSILON = 1e-06
VMEM_LIMIT = 32 * 1024 * 1024

MESH = pl.DeviceIdType.MESH
F32, BF16, I32 = jnp.float32, jnp.bfloat16, jnp.int32
G = 8
NB = 16
TILE = 128
TILES = 32
CH = 64
SUB = CH // G
STRAIGHT, TWO_STEPS = pl.ds(0, 3), pl.ds(3, SUB - 3)


NEAR = {"season": 8, "row": 4, "col": 2}
FAR_FIRST = {
    "season": [(0, 4), (0, 3), (0, 5), (0, 2), (0, 6), (0, 1), (0, 7)],
    "row": [(1, 2), (0, 2), (1, 1), (1, 3), (0, 1), (0, 3), (1, 0)],
    "col": [(2, 0), (2, 1), (1, 0), (3, 0), (1, 1), (3, 1), (0, 1)],
}


def others(axis):
    me, n = lax.axis_index(axis), NEAR[axis]
    i, j = me // n, lax.rem(me, n)
    return [lax.rem(i + a, G // n) * n + lax.rem(j + b, n) for a, b in FAR_FIRST[axis]]


def to_peers(axis, copy):
    for to in others(axis):
        copy(to, {axis: to})


def wait_bytes(ref, sem):
    pltpu.make_async_copy(ref, ref, sem).wait()


def split2(v):
    high = v.astype(BF16)
    return high, (v - high.astype(F32)).astype(BF16)


def first_and_last(keys, other):
    k = lax.broadcasted_iota(I32, (NB, TILES), 1)
    hit = keys == lax.broadcasted_iota(I32, (NB, TILES), 0)
    one = jnp.min(jnp.where(hit, k, TILES - 1), axis=1, keepdims=True)
    two = jnp.max(jnp.where(hit, k, 0), axis=1, keepdims=True)
    pick = lambda t: jnp.sum(jnp.where(k == t, other, 0), axis=1, keepdims=True)
    return one, two, pick(one), pick(two)


def products(order, column, tiles_ref, values_ref, picked, out):
    for b in range(NB):
        picked[b : b + 1, 0:TILE] = values_ref[pl.ds(order[b, column + 2], 1), :]
        picked[b : b + 1, TILE : 2 * TILE] = values_ref[pl.ds(order[b, column + 3], 1), :]
    high, low = split2(picked[...])
    left = jnp.concatenate([high, low], axis=0)
    for b in range(NB):
        right = jnp.concatenate(
            [tiles_ref[order[b, column]], tiles_ref[order[b, column + 1]]], axis=0
        )
        res = jnp.dot(left, right, preferred_element_type=F32)
        row = res[b : b + 1, :] + res[NB + b : NB + b + 1, :]
        out(b, row[:, 0:TILE] + row[:, TILE : 2 * TILE])


def kernel(
    tiles_hbm, rows_hbm, cols_hbm, rhs_hbm, coup_hbm, asset_hbm, costx_hbm, upper_hbm, costz_hbm, x0_hbm, z0_hbm, y0_hbm,
    x_out, z_out, y_out,
    tiles, rows_ref, cols_ref, rhs_ref, coup_ref, asset_ref, costx_ref, upper_ref, costz, xv, zv, yv,
    tb, tf, tr, fw, picked, order_v, order, mask, hot_hi, hot_lo, left,
    gsend, rs, rx, sx, ez, cx, rows_in,
    load_sem, order_sem, send_sem, recv_sem, zs_sem, zr_sem,
):
    s, r, c = (lax.axis_index(a) for a in ("season", "row", "col"))
    barrier = pltpu.get_barrier_semaphore()
    for axis in ("season", "row", "col"):
        for to in others(axis):
            pl.semaphore_signal(barrier, inc=1, device_id={axis: to}, device_id_type=MESH)
    mine = pl.ds(pl.multiple_of(c * CH + r * SUB, SUB), SUB)
    loads = [
        pltpu.make_async_copy(there, here, load_sem.at[k])
        for k, (there, here) in enumerate([
            (asset_hbm, asset_ref), (coup_hbm, coup_ref), (y0_hbm, yv), (rows_hbm, rows_ref), (cols_hbm, cols_ref),
            (tiles_hbm, tiles), (costz_hbm.at[mine], costz), (z0_hbm.at[mine], zv), (x0_hbm, xv),
            (costx_hbm, costx_ref), (upper_hbm, upper_ref), (rhs_hbm, rhs_ref),
        ])
    ]
    for load in loads:
        load.start()

    loads[0].wait()
    asset = asset_ref[...]
    low, high = asset & (TILE - 1), (asset >> 7) - c * CH
    for n in range(NB):
        at = slice(n * TILE, (n + 1) * TILE)
        hit = lax.broadcasted_iota(I32, (TILE, TILE), 0) == low[n : n + 1, :]
        one = jnp.where(hit, 1.0, 0.0).astype(BF16)
        hot_lo[0:TILE, at] = one
        hot_lo[TILE : 2 * TILE, at] = one
        hit = lax.broadcasted_iota(I32, (CH, TILE), 0) == high[n : n + 1, :]
        one = jnp.where(hit, 1.0, 0.0)
        mask[:, at] = one
        hot_hi[:, at] = one.astype(BF16)

    loads[1].wait()
    loads[2].wait()
    coup = coup_ref[...]

    def send_z(k, axis, blocks):
        def send(to, device):
            pltpu.make_async_remote_copy(
                src_ref=blocks, dst_ref=blocks,
                send_sem=zs_sem.at[k], recv_sem=zr_sem.at[k], device_id=device, device_id_type=MESH,
            ).start()

        to_peers(axis, send)

    balance = None
    stats = None
    for it in range(ITERS):
        last = it + 1 == ITERS
        srows = SUB if it == 0 else SUB + 2
        crows = NB if last else NB + 1
        sem = lambda phase: (send_sem.at[it, phase], recv_sem.at[it, phase])

        v_high, v_low = split2(coup * yv[...])
        for n in range(NB):
            at = slice(n * TILE, (n + 1) * TILE)
            hot = hot_hi[:, at]
            left[0:CH, at] = hot * v_high[n : n + 1, :]
            left[CH : 2 * CH, at] = hot * v_low[n : n + 1, :]
        cap = lax.dot_general(
            left[...], hot_lo[0:TILE, :], (((1,), (1,)), ((), ())), preferred_element_type=F32
        )
        cap = cap[0:CH] + cap[CH : 2 * CH]
        for k in range(G):
            gsend[it, k, 0:SUB] = cap[k * SUB : (k + 1) * SUB]
            if it:
                gsend[it, k, SUB : SUB + 2] = stats
        if it == 0:
            pl.semaphore_wait(barrier, 3 * (G - 1))
        sends, recvs = sem(0)

        def send(to, device):
            pltpu.make_async_remote_copy(
                src_ref=gsend.at[it, to, pl.ds(0, srows)], dst_ref=rs.at[it, r, pl.ds(0, srows)],
                send_sem=sends, recv_sem=recvs, device_id=device, device_id_type=MESH,
            ).start()

        to_peers("row", send)
        rs[it, r] = gsend[it, r]

        if it == 0:
            loads[3].wait()
            loads[4].wait()
            rows, cols = rows_ref[...], cols_ref[...]
            place = lax.broadcasted_iota(I32, (NB, TILE), 1)
            table = jnp.zeros((NB, TILE), I32)
            for at, col in enumerate(first_and_last(cols, rows) + first_and_last(rows, cols)):
                table = jnp.where(place == at, col, table)
            order_v[...] = table
            to_smem = pltpu.make_async_copy(order_v, order, order_sem)
            to_smem.start()
            loads[5].wait()
            for k in range(TILES):
                t_high, t_low = split2(tiles[k])
                tb[k, :, 0:TILE] = t_high
                tb[k, :, TILE : 2 * TILE] = t_low
            to_smem.wait()

        def put(b, row):
            rx[it, r, b : b + 1, :] = row

        products(order, 0, tb, yv, picked, put)
        x_sends, x_recvs = sem(1)

        def send(to, device):
            pltpu.make_async_remote_copy(
                src_ref=rx.at[it, r], dst_ref=rx.at[it, r],
                send_sem=x_sends, recv_sem=x_recvs, device_id=device, device_id_type=MESH,
            ).start()

        to_peers("row", send)

        wait_bytes(rs.at[it, pl.ds(0, G - 1), pl.ds(0, srows)], recvs)
        sx[it, s, 0:srows] = jnp.sum(rs[it, :, 0:srows], axis=0)
        sends, recvs = sem(2)

        def send(to, device):
            pltpu.make_async_remote_copy(
                src_ref=sx.at[it, s, pl.ds(0, srows)], dst_ref=sx.at[it, s, pl.ds(0, srows)],
                send_sem=sends, recv_sem=recvs, device_id=device, device_id_type=MESH,
            ).start()

        to_peers("season", send)
        if it == 0:
            for k in range(TILES):
                t_high, t_low = split2(tiles[k].T)
                tf[k, :, 0:TILE] = t_high
                tf[k, :, TILE : 2 * TILE] = t_low
            for load in loads[6:]:
                load.wait()
        wait_bytes(rx.at[it, pl.ds(0, G - 1)], x_recvs)
        transposed = jnp.sum(rx[it], axis=0)
        wait_bytes(sx.at[it, pl.ds(0, G - 1), pl.ds(0, srows)], recvs)
        total = jnp.sum(sx[it, :, 0:srows], axis=0)
        if it == 0:
            primal_step, dual_step = jnp.full((1, 1), STEP_SCALE, F32), jnp.full((1, 1), STEP_SCALE, F32)
        else:
            dual_sq = jnp.sum(total[SUB : SUB + 1], axis=1, keepdims=True)
            primal_sq = jnp.sum(total[SUB + 1 : SUB + 2], axis=1, keepdims=True) * (1.0 / G)
            square = jnp.sqrt(primal_sq + EPSILON) * lax.rsqrt(dual_sq + EPSILON)
            if balance is not None:
                square = balance * square
            balance = jnp.sqrt(square)
            primal_step, dual_step = STEP_SCALE * lax.rsqrt(square), STEP_SCALE * balance

        z_old = zv[...]
        z_new = jnp.maximum(z_old - primal_step * (costz[...] - total[0:SUB]), 0.0)
        zv[...] = z_new
        ez[it, r] = 2.0 * z_new - z_old
        sends, recvs = sem(3)

        def send(to, device):
            pltpu.make_async_remote_copy(
                src_ref=ez.at[it, r], dst_ref=ez.at[it, r],
                send_sem=sends, recv_sem=recvs, device_id=device, device_id_type=MESH,
            ).start()

        to_peers("row", send)
        if last:
            z_out[c, r] = z_new
            send_z(0, "col", z_out.at[c, r, TWO_STEPS])

        x_old = xv[...]
        x_new = jnp.clip(x_old - primal_step * (costx_ref[...] - transposed), 0.0, upper_ref[...])
        xv[...] = x_new
        tr[...] = 2.0 * x_new - x_old

        def put(b, row):
            fw[b : b + 1, :] = row

        products(order, 4, tf, tr, picked, put)
        if last:
            x_out[...] = x_new
            for to_c in [c] + others("col"):
                for to_r in [r] + others("row"):
                    if to_c is not c or to_r is not r:
                        pltpu.make_async_remote_copy(
                            src_ref=z_out.at[c, r, STRAIGHT], dst_ref=z_out.at[c, r, STRAIGHT],
                            send_sem=zs_sem.at[2], recv_sem=zr_sem.at[2],
                            device_id={"row": to_r, "col": to_c}, device_id_type=MESH,
                        ).start()
        else:
            cx[it, c, NB : NB + 1] = jnp.sum((x_new - x_old) ** 2, axis=0, keepdims=True) + jnp.sum(
                (z_new - z_old) ** 2, axis=0, keepdims=True
            )

        wait_bytes(ez.at[it, pl.ds(0, G - 1)], recvs)
        e_high, e_low = split2(ez[it].reshape(CH, TILE))
        gathered = jnp.dot(
            jnp.concatenate([e_high, e_low], axis=1), hot_lo[...], preferred_element_type=F32
        )
        for n in range(NB):
            at = slice(n * TILE, (n + 1) * TILE)
            linked = jnp.sum(gathered[:, at] * mask[:, at], axis=0, keepdims=True)
            cx[it, c, n : n + 1] = fw[n : n + 1, :] + coup[n : n + 1, :] * linked
        sends, recvs = sem(4)

        def send(to, device):
            pltpu.make_async_remote_copy(
                src_ref=cx.at[it, c, pl.ds(0, crows)], dst_ref=cx.at[it, c, pl.ds(0, crows)],
                send_sem=sends, recv_sem=recvs, device_id=device, device_id_type=MESH,
            ).start()

        to_peers("col", send)
        if last:
            wait_bytes(z_out.at[pl.ds(0, G - 1), 0, TWO_STEPS], zr_sem.at[0])
            send_z(1, "row", z_out.at[:, r, TWO_STEPS])
        wait_bytes(cx.at[it, pl.ds(0, G - 1), pl.ds(0, crows)], recvs)
        image = jnp.sum(cx[it, :, 0:crows], axis=0)

        y_old = yv[...]
        y_new = jnp.maximum(y_old + dual_step * (rhs_ref[...] - image[0:NB]), 0.0)
        yv[...] = y_new
        if last:
            y_out[...] = y_new
        else:
            stats = jnp.concatenate(
                [jnp.sum((y_new - y_old) ** 2, axis=0, keepdims=True), image[NB : NB + 1]], axis=0
            )

    wait_bytes(z_out.at[pl.ds(0, G - 1), :, TWO_STEPS], zr_sem.at[1])
    wait_bytes(z_out.at[pl.ds(0, G - 1), 0, TWO_STEPS], zs_sem.at[0])
    wait_bytes(z_out.at[pl.ds(0, G - 1), :, TWO_STEPS], zs_sem.at[1])
    for sem in (zr_sem.at[2], zs_sem.at[2]):
        wait_bytes(rows_in.at[pl.ds(0, 3 * (G * G - 1))], sem)
    for it in range(ITERS):
        srows = SUB if it == 0 else SUB + 2
        crows = NB if it + 1 == ITERS else NB + 1
        wait_bytes(gsend.at[it, pl.ds(0, G - 1), pl.ds(0, srows)], send_sem.at[it, 0])
        wait_bytes(rx.at[it, pl.ds(0, G - 1)], send_sem.at[it, 1])
        wait_bytes(sx.at[it, pl.ds(0, G - 1), pl.ds(0, srows)], send_sem.at[it, 2])
        wait_bytes(ez.at[it, pl.ds(0, G - 1)], send_sem.at[it, 3])
        wait_bytes(cx.at[it, pl.ds(0, G - 1), pl.ds(0, crows)], send_sem.at[it, 4])


def place(x_ref, z_ref, y_ref, x_out, z_out, y_out, sem):
    copies = [
        pltpu.make_async_copy(here, there, sem.at[k])
        for k, (here, there) in enumerate([(z_ref, z_out), (x_ref, x_out), (y_ref, y_out)])
    ]
    for copy in copies:
        copy.start()
    for copy in copies:
        copy.wait()


def local(
    tiles, tile_rows, tile_cols, rhs, coupling, asset, cost_x, upper, cost_z, x_init, z_init, y_init
):
    block = lambda a: a.reshape(NB, TILE)
    inside = pl.BlockSpec(memory_space=pltpu.VMEM)
    in_hbm = lambda a: pltpu.with_memory_space_constraint(a, pltpu.HBM)
    in_vmem = lambda a: pltpu.with_memory_space_constraint(a, pltpu.VMEM)
    operands = (
        tiles.reshape(TILES, TILE, TILE),
        tile_rows.reshape(1, TILES),
        tile_cols.reshape(1, TILES),
        block(rhs),
        block(coupling),
        block(asset),
        block(cost_x),
        block(upper),
        cost_z.reshape(G * CH, TILE),
        block(x_init),
        z_init.reshape(G * CH, TILE),
        block(y_init),
    )
    x, z, y = pl.pallas_call(
        kernel,
        out_shape=(
            pltpu.VMEM((NB, TILE), F32), pltpu.VMEM((G, G, SUB, TILE), F32), pltpu.VMEM((NB, TILE), F32),
        ),
        in_specs=[pl.BlockSpec(memory_space=pltpu.HBM)] * 12,
        out_specs=(inside, inside, inside),
        scratch_shapes=[
            pltpu.VMEM((TILES, TILE, TILE), F32),
            pltpu.VMEM((1, TILES), I32),
            pltpu.VMEM((1, TILES), I32),
            pltpu.VMEM((NB, TILE), F32),
            pltpu.VMEM((NB, TILE), F32),
            pltpu.VMEM((NB, TILE), I32),
            pltpu.VMEM((NB, TILE), F32),
            pltpu.VMEM((NB, TILE), F32),
            pltpu.VMEM((SUB, TILE), F32),
            pltpu.VMEM((NB, TILE), F32),
            pltpu.VMEM((SUB, TILE), F32),
            pltpu.VMEM((NB, TILE), F32),
            pltpu.VMEM((TILES, TILE, 2 * TILE), BF16),
            pltpu.VMEM((TILES, TILE, 2 * TILE), BF16),
            pltpu.VMEM((NB, TILE), F32),
            pltpu.VMEM((NB, TILE), F32),
            pltpu.VMEM((NB, 2 * TILE), F32),
            pltpu.VMEM((NB, TILE), I32),
            pltpu.SMEM((NB, TILE), I32),
            pltpu.VMEM((CH, NB * TILE), F32),
            pltpu.VMEM((CH, NB * TILE), BF16),
            pltpu.VMEM((2 * TILE, NB * TILE), BF16),
            pltpu.VMEM((2 * CH, NB * TILE), BF16),
            pltpu.VMEM((ITERS, G, SUB + 2, TILE), F32),
            pltpu.VMEM((ITERS, G, SUB + 2, TILE), F32),
            pltpu.VMEM((ITERS, G, NB, TILE), F32),
            pltpu.VMEM((ITERS, G, SUB + 2, TILE), F32),
            pltpu.VMEM((ITERS, G, SUB, TILE), F32),
            pltpu.VMEM((ITERS, G, NB + 1, TILE), F32),
            pltpu.VMEM((3 * G * G, TILE), F32),
            pltpu.SemaphoreType.DMA((12,)),
            pltpu.SemaphoreType.DMA,
            pltpu.SemaphoreType.DMA((ITERS, 5)),
            pltpu.SemaphoreType.DMA((ITERS, 5)),
            pltpu.SemaphoreType.DMA((3,)),
            pltpu.SemaphoreType.DMA((3,)),
        ],
        compiler_params=pltpu.CompilerParams(
            collective_id=0, has_side_effects=True, vmem_limit_bytes=VMEM_LIMIT
        ),
    )(*map(in_hbm, operands))
    x, z, y = pl.pallas_call(
        place,
        out_shape=tuple(jax.ShapeDtypeStruct(a.shape, F32) for a in (x, z, y)),
        in_specs=[inside] * 3,
        out_specs=(pl.BlockSpec(memory_space=pl.ANY),) * 3,
        scratch_shapes=[pltpu.SemaphoreType.DMA((3,))],
    )(*map(in_vmem, (x, z, y)))
    return x.reshape(1, -1), z.reshape(-1), y.reshape(1, -1)


def solution(mesh):
    in_specs = (
        P("season", "row", "col", None, None, None),
        P("season", "row", "col", None),
        P("season", "row", "col", None),
        P("season", "row"),
        P("season", "row"),
        P("season", "row"),
        P("season", "col"),
        P("season", "col"),
        P(),
        P("season", "col"),
        P(),
        P("season", "row"),
    )
    out_specs = (P("season", "col"), P(), P("season", "row"))
    return jax.shard_map(local, mesh=mesh, in_specs=in_specs, out_specs=out_specs, check_vma=False)
```

```python
import functools

import jax
import jax.numpy as jnp
from jax import lax
from jax.experimental import pallas as pl
from jax.experimental.pallas import tpu as pltpu
from jax.sharding import PartitionSpec as P

ITERS = 3
STEP_SCALE = 0.35
EPSILON = 1e-06
VMEM_LIMIT = 32 * 1024 * 1024

MESH = pl.DeviceIdType.MESH
F32, BF16, I32 = jnp.float32, jnp.bfloat16, jnp.int32
G = 8
NB = 16
TILE = 128
TILES = 32
CH = 64
SUB = CH // G
EARLY = 4
STRAIGHT, TWO_STEPS = pl.ds(0, 3), pl.ds(3, SUB - 3)


NEAR = {"season": 8, "row": 4, "col": 2}
FAR_FIRST = {
    "season": [(0, 4), (0, 3), (0, 5), (0, 2), (0, 6), (0, 1), (0, 7)],
    "row": [(1, 2), (0, 2), (1, 1), (1, 3), (0, 1), (0, 3), (1, 0)],
    "col": [(2, 0), (2, 1), (1, 0), (3, 0), (1, 1), (3, 1), (0, 1)],
}


def others(axis):
    me, n = lax.axis_index(axis), NEAR[axis]
    i, j = me // n, lax.rem(me, n)
    return [lax.rem(i + a, G // n) * n + lax.rem(j + b, n) for a, b in FAR_FIRST[axis]]


def to_peers(axis, copy):
    for to in others(axis):
        copy(to, {axis: to})


def wait_bytes(ref, sem):
    pltpu.make_async_copy(ref, ref, sem).wait()


def split2(v):
    high = v.astype(BF16)
    return high, (v - high.astype(F32)).astype(BF16)


def first_and_last(keys, other):
    k = lax.broadcasted_iota(I32, (NB, TILES), 1)
    hit = keys == lax.broadcasted_iota(I32, (NB, TILES), 0)
    one = jnp.min(jnp.where(hit, k, TILES - 1), axis=1, keepdims=True)
    two = jnp.max(jnp.where(hit, k, 0), axis=1, keepdims=True)
    pick = lambda t: jnp.sum(jnp.where(k == t, other, 0), axis=1, keepdims=True)
    return one, two, pick(one), pick(two)


def products(order, column, tiles_ref, values_ref, picked, out):
    for b in range(NB):
        picked[b : b + 1, 0:TILE] = values_ref[pl.ds(order[b, column + 2], 1), :]
        picked[b : b + 1, TILE : 2 * TILE] = values_ref[pl.ds(order[b, column + 3], 1), :]
    high, low = split2(picked[...])
    left = jnp.concatenate([high, low], axis=0)
    for b in range(NB):
        right = jnp.concatenate(
            [tiles_ref[order[b, column]], tiles_ref[order[b, column + 1]]], axis=0
        )
        res = jnp.dot(left, right, preferred_element_type=F32)
        row = res[b : b + 1, :] + res[NB + b : NB + b + 1, :]
        out(b, row[:, 0:TILE] + row[:, TILE : 2 * TILE])


def kernel(
    tiles_hbm, rows_hbm, cols_hbm, rhs_hbm, coup_hbm, asset_hbm, costx_hbm, upper_hbm, costz_hbm, x0_hbm, z0_hbm, y0_hbm,
    x_out, z_out, y_out,
    tiles, rows_ref, cols_ref, rhs_ref, coup_ref, asset_ref, costx_ref, upper_ref, costz, xv, zv, yv,
    costz_pair, z_pair, z_in, tb, tf, tr, fw, picked, order_v, order, mask, hot_hi, hot_lo, left,
    gsend, rs, rx, sx, ez, cx, rows_in,
    load_sem, order_sem, send_sem, recv_sem, zs_sem, zr_sem, pair_sem, here_sem,
):
    s, r, c = (lax.axis_index(a) for a in ("season", "row", "col"))
    barrier = pltpu.get_barrier_semaphore()
    early, late = c < EARLY, c >= EARLY
    for axis in ("season", "row"):
        for to in others(axis):
            pl.semaphore_signal(barrier, inc=1, device_id={axis: to}, device_id_type=MESH)
    for to in others("col"):
        @pl.when(jnp.logical_or(early, to >= EARLY))
        def _():
            pl.semaphore_signal(barrier, inc=1, device_id={"col": to}, device_id_type=MESH)

    mine = pl.ds(pl.multiple_of(c * CH + r * SUB, SUB), SUB)
    pair = pl.ds(pl.multiple_of(lax.rem(c + EARLY, G) * CH + r * SUB, SUB), SUB)
    loads = [
        pltpu.make_async_copy(there, here, load_sem.at[k])
        for k, (there, here) in enumerate([
            (asset_hbm, asset_ref), (coup_hbm, coup_ref), (y0_hbm, yv), (rows_hbm, rows_ref), (cols_hbm, cols_ref),
            (tiles_hbm, tiles), (costz_hbm.at[mine], costz), (z0_hbm.at[mine], zv), (x0_hbm, xv),
            (costx_hbm, costx_ref), (upper_hbm, upper_ref), (rhs_hbm, rhs_ref),
            (costz_hbm.at[pair], costz_pair), (z0_hbm.at[pair], z_pair),
        ])
    ]
    for load in loads:
        load.start()

    loads[0].wait()
    asset = asset_ref[...]
    low, high = asset & (TILE - 1), (asset >> 7) - c * CH
    high_pair = high - EARLY * CH
    for n in range(NB):
        at = slice(n * TILE, (n + 1) * TILE)
        hit = lax.broadcasted_iota(I32, (TILE, TILE), 0) == low[n : n + 1, :]
        one = jnp.where(hit, 1.0, 0.0).astype(BF16)
        hot_lo[0:TILE, at] = one
        hot_lo[TILE : 2 * TILE, at] = one
        hit = lax.broadcasted_iota(I32, (CH, TILE), 0) == high[n : n + 1, :]
        one = jnp.where(hit, 1.0, 0.0)
        mask[0, :, at] = one
        hot_hi[0, :, at] = one.astype(BF16)

    @pl.when(early)
    def _():
        for n in range(NB):
            at = slice(n * TILE, (n + 1) * TILE)
            hit = lax.broadcasted_iota(I32, (CH, TILE), 0) == high_pair[n : n + 1, :]
            one = jnp.where(hit, 1.0, 0.0)
            mask[1, :, at] = one
            hot_hi[1, :, at] = one.astype(BF16)

    loads[1].wait()
    loads[2].wait()
    coup = coup_ref[...]

    def spread(axis, blocks, send, recv):
        def start(to, device):
            pltpu.make_async_remote_copy(
                src_ref=blocks, dst_ref=blocks, send_sem=send, recv_sem=recv, device_id=device, device_id_type=MESH
            ).start()

        to_peers(axis, start)

    def z_to_pair(to):
        return pltpu.make_async_remote_copy(
            src_ref=z_pair, dst_ref=z_in, send_sem=pair_sem.at[0], recv_sem=pair_sem.at[1],
            device_id={"col": to}, device_id_type=MESH,
        )

    def send_z(k, axis, blocks):
        spread(axis, blocks, zs_sem.at[k], zr_sem.at[k])

    def investment(k):
        v_high, v_low = split2(coup * yv[...])
        for n in range(NB):
            at = slice(n * TILE, (n + 1) * TILE)
            hot = hot_hi[k, :, at]
            left[k, 0:CH, at] = hot * v_high[n : n + 1, :]
            left[k, CH : 2 * CH, at] = hot * v_low[n : n + 1, :]
        cap = lax.dot_general(
            left[k], hot_lo[0:TILE, :], (((1,), (1,)), ((), ())), preferred_element_type=F32
        )
        return cap[0:CH] + cap[CH : 2 * CH]

    def linked(k, values):
        e_high, e_low = split2(values)
        gathered = jnp.dot(
            jnp.concatenate([e_high, e_low], axis=1), hot_lo[...], preferred_element_type=F32
        )
        for n in range(NB):
            at = slice(n * TILE, (n + 1) * TILE)
            yield n, coup[n : n + 1, :] * jnp.sum(gathered[:, at] * mask[k, :, at], axis=0, keepdims=True)

    balance = None
    stats = None
    for it in range(ITERS):
        last = it + 1 == ITERS
        srows = 2 * SUB if it == 0 else SUB + 2
        crows = NB if last else NB + 1
        sem = lambda phase: (send_sem.at[it, phase], recv_sem.at[it, phase])

        def send_sums(to, device):
            pltpu.make_async_remote_copy(
                src_ref=gsend.at[it, to, pl.ds(0, srows)], dst_ref=rs.at[it, r, pl.ds(0, srows)],
                send_sem=send_sem.at[it, 0], recv_sem=recv_sem.at[it, 0], device_id=device, device_id_type=MESH,
            ).start()

        if it == 0:

            @pl.when(early)
            def _():
                for half in range(2):
                    cap = investment(half)
                    for k in range(G):
                        gsend[0, k, half * SUB : (half + 1) * SUB] = cap[k * SUB : (k + 1) * SUB]

        else:
            cap = investment(0)
            for k in range(G):
                gsend[it, k, 0:SUB] = cap[k * SUB : (k + 1) * SUB]
                gsend[it, k, SUB : SUB + 2] = stats
            to_peers("row", send_sums)
            rs[it, r] = gsend[it, r]

        if it == 0:
            loads[3].wait()
            loads[4].wait()
            rows, cols = rows_ref[...], cols_ref[...]
            place = lax.broadcasted_iota(I32, (NB, TILE), 1)
            table = jnp.zeros((NB, TILE), I32)
            for at, col in enumerate(first_and_last(cols, rows) + first_and_last(rows, cols)):
                table = jnp.where(place == at, col, table)
            order_v[...] = table
            to_smem = pltpu.make_async_copy(order_v, order, order_sem)
            to_smem.start()
            loads[5].wait()
            for k in range(TILES):
                t_high, t_low = split2(tiles[k])
                tb[k, :, 0:TILE] = t_high
                tb[k, :, TILE : 2 * TILE] = t_low
            to_smem.wait()

        def put(b, row):
            rx[it, r, b : b + 1, :] = row

        products(order, 0, tb, yv, picked, put)
        if it == 0:

            @pl.when(early)
            def _():
                pl.semaphore_wait(barrier, 2 * (G - 1) + EARLY - 1)
                to_peers("row", send_sums)
                rs[0, r] = gsend[0, r]

            @pl.when(late)
            def _():
                pl.semaphore_wait(barrier, 3 * (G - 1))
                for to in range(EARLY):
                    pl.semaphore_signal(here_sem, inc=1, device_id={"col": to}, device_id_type=MESH)

        spread("row", rx.at[it, r], *sem(1))

        def sum_rows():
            wait_bytes(rs.at[it, pl.ds(0, G - 1), pl.ds(0, srows)], recv_sem.at[it, 0])
            sx[it, s, 0:srows] = jnp.sum(rs[it, :, 0:srows], axis=0)
            spread("season", sx.at[it, s, pl.ds(0, srows)], *sem(2))

        def sum_seasons():
            wait_bytes(sx.at[it, pl.ds(0, G - 1), pl.ds(0, srows)], recv_sem.at[it, 2])
            return jnp.sum(sx[it, :, 0:srows], axis=0)

        if it == 0:
            pl.when(early)(sum_rows)
            for k in range(TILES):
                t_high, t_low = split2(tiles[k].T)
                tf[k, :, 0:TILE] = t_high
                tf[k, :, TILE : 2 * TILE] = t_low
            for load in loads[6:]:
                load.wait()
        else:
            sum_rows()
        wait_bytes(rx.at[it, pl.ds(0, G - 1)], recv_sem.at[it, 1])
        transposed = jnp.sum(rx[it], axis=0)
        if it == 0:
            primal_step, dual_step = jnp.full((1, 1), STEP_SCALE, F32), jnp.full((1, 1), STEP_SCALE, F32)
        else:
            total = sum_seasons()
            dual_sq = jnp.sum(total[SUB : SUB + 1], axis=1, keepdims=True)
            primal_sq = jnp.sum(total[SUB + 1 : SUB + 2], axis=1, keepdims=True) * (1.0 / G)
            square = jnp.sqrt(primal_sq + EPSILON) * lax.rsqrt(dual_sq + EPSILON)
            if balance is not None:
                square = balance * square
            balance = jnp.sqrt(square)
            primal_step, dual_step = STEP_SCALE * lax.rsqrt(square), STEP_SCALE * balance
            if it == 1:
                @pl.when(late)
                def _():
                    wait_bytes(z_in, pair_sem.at[1])
                    zv[...] = z_in[...]

            z_old = zv[...]
            z_new = jnp.maximum(z_old - primal_step * (costz[...] - total[0:SUB]), 0.0)
            zv[...] = z_new
            ez[it, r, 0:SUB] = 2.0 * z_new - z_old
            spread("row", ez.at[it, r, pl.ds(0, SUB)], *sem(3))
            z_change = jnp.sum((z_new - z_old) ** 2, axis=0, keepdims=True)
        if last:
            z_out[c, r] = z_new
            send_z(0, "col", z_out.at[c, r, TWO_STEPS])

        x_old = xv[...]
        x_new = jnp.clip(x_old - primal_step * (costx_ref[...] - transposed), 0.0, upper_ref[...])
        xv[...] = x_new
        tr[...] = 2.0 * x_new - x_old

        def put(b, row):
            fw[b : b + 1, :] = row

        products(order, 4, tf, tr, picked, put)
        if last:
            x_out[...] = x_new
            for to_c in [c] + others("col"):
                for to_r in [r] + others("row"):
                    if to_c is not c or to_r is not r:
                        pltpu.make_async_remote_copy(
                            src_ref=z_out.at[c, r, STRAIGHT], dst_ref=z_out.at[c, r, STRAIGHT],
                            send_sem=zs_sem.at[2], recv_sem=zr_sem.at[2],
                            device_id={"row": to_r, "col": to_c}, device_id_type=MESH,
                        ).start()
        x_change = jnp.sum((x_new - x_old) ** 2, axis=0, keepdims=True)

        if it == 0:

            @pl.when(early)
            def _():
                total = sum_seasons()
                z_old = jnp.concatenate([zv[...], z_pair[...]], axis=0)
                cost = jnp.concatenate([costz[...], costz_pair[...]], axis=0)
                z_new = jnp.maximum(z_old - STEP_SCALE * (cost - total), 0.0)
                zv[...] = z_new[0:SUB]
                z_pair[...] = z_new[SUB : 2 * SUB]
                ez[0, r] = 2.0 * z_new - z_old
                spread("row", ez.at[0, r], *sem(3))
                cx[0, c, NB : NB + 1] = x_change + jnp.sum((z_new - z_old) ** 2, axis=0, keepdims=True)
                pl.semaphore_wait(here_sem, G - EARLY)
                z_to_pair(c + EARLY).start()
                wait_bytes(ez.at[0, pl.ds(0, G - 1)], recv_sem.at[0, 3])
                for (n, one), (_, two) in zip(
                    linked(0, ez[0, :, 0:SUB].reshape(CH, TILE)),
                    linked(1, ez[0, :, SUB : 2 * SUB].reshape(CH, TILE)),
                ):
                    cx[0, c, n : n + 1] = fw[n : n + 1, :] + (one + two)

            @pl.when(late)
            def _():
                cx[0, c, 0:NB] = fw[...]
                cx[0, c, NB : NB + 1] = x_change

        else:
            if not last:
                cx[it, c, NB : NB + 1] = x_change + z_change
            wait_bytes(ez.at[it, pl.ds(0, G - 1), pl.ds(0, SUB)], recv_sem.at[it, 3])
            for n, one in linked(0, ez[it, :, 0:SUB].reshape(CH, TILE)):
                cx[it, c, n : n + 1] = fw[n : n + 1, :] + one
        spread("col", cx.at[it, c, pl.ds(0, crows)], *sem(4))
        if last:
            wait_bytes(z_out.at[pl.ds(0, G - 1), 0, TWO_STEPS], zr_sem.at[0])
            send_z(1, "row", z_out.at[:, r, TWO_STEPS])
        wait_bytes(cx.at[it, pl.ds(0, G - 1), pl.ds(0, crows)], recv_sem.at[it, 4])
        image = jnp.sum(cx[it, :, 0:crows], axis=0)

        y_old = yv[...]
        y_new = jnp.maximum(y_old + dual_step * (rhs_ref[...] - image[0:NB]), 0.0)
        yv[...] = y_new
        if last:
            y_out[...] = y_new
        else:
            stats = jnp.concatenate(
                [jnp.sum((y_new - y_old) ** 2, axis=0, keepdims=True), image[NB : NB + 1]], axis=0
            )

    wait_bytes(z_out.at[pl.ds(0, G - 1), :, TWO_STEPS], zr_sem.at[1])
    wait_bytes(z_out.at[pl.ds(0, G - 1), 0, TWO_STEPS], zs_sem.at[0])
    wait_bytes(z_out.at[pl.ds(0, G - 1), :, TWO_STEPS], zs_sem.at[1])
    for sem in (zr_sem.at[2], zs_sem.at[2]):
        wait_bytes(rows_in.at[pl.ds(0, 3 * (G * G - 1))], sem)
    for it in range(ITERS):
        srows = 2 * SUB if it == 0 else SUB + 2
        erows = 2 * SUB if it == 0 else SUB
        crows = NB if it + 1 == ITERS else NB + 1

        def sent():
            wait_bytes(gsend.at[it, pl.ds(0, G - 1), pl.ds(0, srows)], send_sem.at[it, 0])
            wait_bytes(sx.at[it, pl.ds(0, G - 1), pl.ds(0, srows)], send_sem.at[it, 2])
            wait_bytes(ez.at[it, pl.ds(0, G - 1), pl.ds(0, erows)], send_sem.at[it, 3])
            if it == 0:
                z_to_pair(c + EARLY).wait_send()

        if it == 0:
            pl.when(early)(sent)
        else:
            sent()
        wait_bytes(rx.at[it, pl.ds(0, G - 1)], send_sem.at[it, 1])
        wait_bytes(cx.at[it, pl.ds(0, G - 1), pl.ds(0, crows)], send_sem.at[it, 4])


def place(x_ref, z_ref, y_ref, x_out, z_out, y_out, sem):
    copies = [
        pltpu.make_async_copy(here, there, sem.at[k])
        for k, (here, there) in enumerate([(z_ref, z_out), (x_ref, x_out), (y_ref, y_out)])
    ]
    for copy in copies:
        copy.start()
    for copy in copies:
        copy.wait()


def local(
    tiles, tile_rows, tile_cols, rhs, coupling, asset, cost_x, upper, cost_z, x_init, z_init, y_init
):
    block = lambda a: a.reshape(NB, TILE)
    inside = pl.BlockSpec(memory_space=pltpu.VMEM)
    in_hbm = lambda a: pltpu.with_memory_space_constraint(a, pltpu.HBM)
    in_vmem = lambda a: pltpu.with_memory_space_constraint(a, pltpu.VMEM)
    operands = (
        tiles.reshape(TILES, TILE, TILE),
        tile_rows.reshape(1, TILES),
        tile_cols.reshape(1, TILES),
        block(rhs),
        block(coupling),
        block(asset),
        block(cost_x),
        block(upper),
        cost_z.reshape(G * CH, TILE),
        block(x_init),
        z_init.reshape(G * CH, TILE),
        block(y_init),
    )
    x, z, y = pl.pallas_call(
        kernel,
        out_shape=(
            pltpu.VMEM((NB, TILE), F32), pltpu.VMEM((G, G, SUB, TILE), F32), pltpu.VMEM((NB, TILE), F32),
        ),
        in_specs=[pl.BlockSpec(memory_space=pltpu.HBM)] * 12,
        out_specs=(inside, inside, inside),
        scratch_shapes=[
            pltpu.VMEM((TILES, TILE, TILE), F32),
            pltpu.VMEM((1, TILES), I32),
            pltpu.VMEM((1, TILES), I32),
            pltpu.VMEM((NB, TILE), F32),
            pltpu.VMEM((NB, TILE), F32),
            pltpu.VMEM((NB, TILE), I32),
            pltpu.VMEM((NB, TILE), F32),
            pltpu.VMEM((NB, TILE), F32),
            pltpu.VMEM((SUB, TILE), F32),
            pltpu.VMEM((NB, TILE), F32),
            pltpu.VMEM((SUB, TILE), F32),
            pltpu.VMEM((NB, TILE), F32),
            pltpu.VMEM((SUB, TILE), F32),
            pltpu.VMEM((SUB, TILE), F32),
            pltpu.VMEM((SUB, TILE), F32),
            pltpu.VMEM((TILES, TILE, 2 * TILE), BF16),
            pltpu.VMEM((TILES, TILE, 2 * TILE), BF16),
            pltpu.VMEM((NB, TILE), F32),
            pltpu.VMEM((NB, TILE), F32),
            pltpu.VMEM((NB, 2 * TILE), F32),
            pltpu.VMEM((NB, TILE), I32),
            pltpu.SMEM((NB, TILE), I32),
            pltpu.VMEM((2, CH, NB * TILE), F32),
            pltpu.VMEM((2, CH, NB * TILE), BF16),
            pltpu.VMEM((2 * TILE, NB * TILE), BF16),
            pltpu.VMEM((2, 2 * CH, NB * TILE), BF16),
            pltpu.VMEM((ITERS, G, 2 * SUB, TILE), F32),
            pltpu.VMEM((ITERS, G, 2 * SUB, TILE), F32),
            pltpu.VMEM((ITERS, G, NB, TILE), F32),
            pltpu.VMEM((ITERS, G, 2 * SUB, TILE), F32),
            pltpu.VMEM((ITERS, G, 2 * SUB, TILE), F32),
            pltpu.VMEM((ITERS, G, NB + 1, TILE), F32),
            pltpu.VMEM((3 * G * G, TILE), F32),
            pltpu.SemaphoreType.DMA((14,)),
            pltpu.SemaphoreType.DMA,
            pltpu.SemaphoreType.DMA((ITERS, 5)),
            pltpu.SemaphoreType.DMA((ITERS, 5)),
            pltpu.SemaphoreType.DMA((3,)),
            pltpu.SemaphoreType.DMA((3,)),
            pltpu.SemaphoreType.DMA((2,)),
            pltpu.SemaphoreType.REGULAR,
        ],
        compiler_params=pltpu.CompilerParams(
            collective_id=0, has_side_effects=True, vmem_limit_bytes=VMEM_LIMIT
        ),
    )(*map(in_hbm, operands))
    x, z, y = pl.pallas_call(
        place,
        out_shape=tuple(jax.ShapeDtypeStruct(a.shape, F32) for a in (x, z, y)),
        in_specs=[inside] * 3,
        out_specs=(pl.BlockSpec(memory_space=pl.ANY),) * 3,
        scratch_shapes=[pltpu.SemaphoreType.DMA((3,))],
    )(*map(in_vmem, (x, z, y)))
    return x.reshape(1, -1), z.reshape(-1), y.reshape(1, -1)


def solution(mesh):
    in_specs = (
        P("season", "row", "col", None, None, None),
        P("season", "row", "col", None),
        P("season", "row", "col", None),
        P("season", "row"),
        P("season", "row"),
        P("season", "row"),
        P("season", "col"),
        P("season", "col"),
        P(),
        P("season", "col"),
        P(),
        P("season", "row"),
    )
    out_specs = (P("season", "col"), P(), P("season", "row"))
    return jax.shard_map(local, mesh=mesh, in_specs=in_specs, out_specs=out_specs, check_vma=False)
```

```python
import functools

import jax
import jax.numpy as jnp
from jax import lax
from jax.experimental import pallas as pl
from jax.experimental.pallas import tpu as pltpu
from jax.sharding import PartitionSpec as P

ITERS = 3
STEP_SCALE = 0.35
EPSILON = 1e-06
VMEM_LIMIT = 32 * 1024 * 1024

MESH = pl.DeviceIdType.MESH
F32, BF16, I32 = jnp.float32, jnp.bfloat16, jnp.int32
G = 8
NB = 16
TILE = 128
TILES = 32
CH = 64
SUB = CH // G
EARLY = 2
SHARE = G // EARLY
STRAIGHT, TWO_STEPS = pl.ds(0, 3), pl.ds(3, SUB - 3)


NEAR = {"season": 8, "row": 4, "col": 2}
FAR_FIRST = {
    "season": [(0, 4), (0, 3), (0, 5), (0, 2), (0, 6), (0, 1), (0, 7)],
    "row": [(1, 2), (0, 2), (1, 1), (1, 3), (0, 1), (0, 3), (1, 0)],
    "col": [(2, 0), (2, 1), (1, 0), (3, 0), (1, 1), (3, 1), (0, 1)],
}


def others(axis):
    me, n = lax.axis_index(axis), NEAR[axis]
    i, j = me // n, lax.rem(me, n)
    return [lax.rem(i + a, G // n) * n + lax.rem(j + b, n) for a, b in FAR_FIRST[axis]]


def to_peers(axis, copy):
    for to in others(axis):
        copy(to, {axis: to})


def wait_bytes(ref, sem):
    pltpu.make_async_copy(ref, ref, sem).wait()


def split2(v):
    high = v.astype(BF16)
    return high, (v - high.astype(F32)).astype(BF16)


def first_and_last(keys, other):
    k = lax.broadcasted_iota(I32, (NB, TILES), 1)
    hit = keys == lax.broadcasted_iota(I32, (NB, TILES), 0)
    one = jnp.min(jnp.where(hit, k, TILES - 1), axis=1, keepdims=True)
    two = jnp.max(jnp.where(hit, k, 0), axis=1, keepdims=True)
    pick = lambda t: jnp.sum(jnp.where(k == t, other, 0), axis=1, keepdims=True)
    return one, two, pick(one), pick(two)


def products(order, column, tiles_ref, values_ref, picked, out):
    for b in range(NB):
        picked[b : b + 1, 0:TILE] = values_ref[pl.ds(order[b, column + 2], 1), :]
        picked[b : b + 1, TILE : 2 * TILE] = values_ref[pl.ds(order[b, column + 3], 1), :]
    high, low = split2(picked[...])
    left = jnp.concatenate([high, low], axis=0)
    for b in range(NB):
        right = jnp.concatenate(
            [tiles_ref[order[b, column]], tiles_ref[order[b, column + 1]]], axis=0
        )
        res = jnp.dot(left, right, preferred_element_type=F32)
        row = res[b : b + 1, :] + res[NB + b : NB + b + 1, :]
        out(b, row[:, 0:TILE] + row[:, TILE : 2 * TILE])


def kernel(
    tiles_hbm, rows_hbm, cols_hbm, rhs_hbm, coup_hbm, asset_hbm, costx_hbm, upper_hbm, costz_hbm, x0_hbm, z0_hbm, y0_hbm,
    x_out, z_out, y_out,
    tiles, rows_ref, cols_ref, rhs_ref, coup_ref, asset_ref, costx_ref, upper_ref, costz, xv, zv, yv,
    costz_more, z_more, z_in, tb, tf, tr, fw, picked, order_v, order, mask, hot_hi, hot_lo, left,
    gsend, rs, rx, sx, ez, cx, rows_in,
    load_sem, order_sem, send_sem, recv_sem, zs_sem, zr_sem, pair_sem, here_sem, far_sem,
):
    s, r, c = (lax.axis_index(a) for a in ("season", "row", "col"))
    barrier = pltpu.get_barrier_semaphore()
    early, late = c < EARLY, c >= EARLY
    at_two = [lax.rem(s + k, G) for k in (2, G - 2)]
    near = at_two + [lax.rem(s + k, G) for k in (1, G - 1)]
    for axis, peers in (("season", near), ("row", others("row"))):
        for to in peers:
            pl.semaphore_signal(barrier, inc=1, device_id={axis: to}, device_id_type=MESH)
    for to in others("col"):
        @pl.when(jnp.logical_or(early, to >= EARLY))
        def _():
            pl.semaphore_signal(barrier, inc=1, device_id={"col": to}, device_id_type=MESH)

    mine = pl.ds(pl.multiple_of(c * CH + r * SUB, SUB), SUB)
    more = [pl.ds(pl.multiple_of(lax.rem(c + EARLY * k, G) * CH + r * SUB, SUB), SUB) for k in range(1, SHARE)]
    loads = [
        pltpu.make_async_copy(there, here, load_sem.at[k])
        for k, (there, here) in enumerate([
            (asset_hbm, asset_ref), (coup_hbm, coup_ref), (y0_hbm, yv), (rows_hbm, rows_ref), (cols_hbm, cols_ref),
            (tiles_hbm, tiles), (costz_hbm.at[mine], costz), (z0_hbm.at[mine], zv), (x0_hbm, xv),
            (costx_hbm, costx_ref), (upper_hbm, upper_ref), (rhs_hbm, rhs_ref),
        ] + [(costz_hbm.at[at], costz_more.at[k]) for k, at in enumerate(more)]
          + [(z0_hbm.at[at], z_more.at[k]) for k, at in enumerate(more)])
    ]
    for load in loads:
        load.start()

    loads[0].wait()
    asset = asset_ref[...]
    low, high = asset & (TILE - 1), (asset >> 7) - c * CH
    for n in range(NB):
        at = slice(n * TILE, (n + 1) * TILE)
        hit = lax.broadcasted_iota(I32, (TILE, TILE), 0) == low[n : n + 1, :]
        one = jnp.where(hit, 1.0, 0.0).astype(BF16)
        hot_lo[0:TILE, at] = one
        hot_lo[TILE : 2 * TILE, at] = one
        hit = lax.broadcasted_iota(I32, (CH, TILE), 0) == high[n : n + 1, :]
        one = jnp.where(hit, 1.0, 0.0)
        mask[0, :, at] = one
        hot_hi[0, :, at] = one.astype(BF16)

    @pl.when(early)
    def _():
        for k in range(1, SHARE):
            for n in range(NB):
                at = slice(n * TILE, (n + 1) * TILE)
                hit = lax.broadcasted_iota(I32, (CH, TILE), 0) == high[n : n + 1, :] - k * EARLY * CH
                one = jnp.where(hit, 1.0, 0.0)
                mask[k, :, at] = one
                hot_hi[k, :, at] = one.astype(BF16)

    loads[1].wait()
    loads[2].wait()
    coup = coup_ref[...]

    def spread(axis, blocks, send, recv):
        def start(to, device):
            pltpu.make_async_remote_copy(
                src_ref=blocks, dst_ref=blocks, send_sem=send, recv_sem=recv, device_id=device, device_id_type=MESH
            ).start()

        to_peers(axis, start)

    def z_to(k):
        return pltpu.make_async_remote_copy(
            src_ref=z_more.at[k - 1], dst_ref=z_in, send_sem=pair_sem.at[k], recv_sem=pair_sem.at[0],
            device_id={"col": c + k * EARLY}, device_id_type=MESH,
        )

    def send_z(k, axis, blocks):
        spread(axis, blocks, zs_sem.at[k], zr_sem.at[k])

    def vouch():
        for to in at_two:
            pl.semaphore_signal(far_sem, inc=1, device_id={"season": to}, device_id_type=MESH)

    def investment(k):
        v_high, v_low = split2(coup * yv[...])
        for n in range(NB):
            at = slice(n * TILE, (n + 1) * TILE)
            hot = hot_hi[k, :, at]
            left[k, 0:CH, at] = hot * v_high[n : n + 1, :]
            left[k, CH : 2 * CH, at] = hot * v_low[n : n + 1, :]
        cap = lax.dot_general(
            left[k], hot_lo[0:TILE, :], (((1,), (1,)), ((), ())), preferred_element_type=F32
        )
        return cap[0:CH] + cap[CH : 2 * CH]

    def linked(k, values):
        e_high, e_low = split2(values)
        gathered = jnp.dot(
            jnp.concatenate([e_high, e_low], axis=1), hot_lo[...], preferred_element_type=F32
        )
        for n in range(NB):
            at = slice(n * TILE, (n + 1) * TILE)
            yield n, coup[n : n + 1, :] * jnp.sum(gathered[:, at] * mask[k, :, at], axis=0, keepdims=True)

    balance = None
    stats = None
    for it in range(ITERS):
        last = it + 1 == ITERS
        srows = SHARE * SUB if it == 0 else SUB + 2
        crows = NB if last else NB + 1
        sem = lambda phase: (send_sem.at[it, phase], recv_sem.at[it, phase])

        def send_sums(to, device):
            pltpu.make_async_remote_copy(
                src_ref=gsend.at[it, to, pl.ds(0, srows)], dst_ref=rs.at[it, r, pl.ds(0, srows)],
                send_sem=send_sem.at[it, 0], recv_sem=recv_sem.at[it, 0], device_id=device, device_id_type=MESH,
            ).start()

        if it == 0:

            @pl.when(early)
            def _():
                for half in range(SHARE):
                    cap = investment(half)
                    for k in range(G):
                        gsend[0, k, half * SUB : (half + 1) * SUB] = cap[k * SUB : (k + 1) * SUB]
                pl.semaphore_wait(barrier, len(near) + G - 1 + EARLY - 1)
                vouch()
                to_peers("row", send_sums)
                rs[0, r] = gsend[0, r]

        else:
            cap = investment(0)
            for k in range(G):
                gsend[it, k, 0:SUB] = cap[k * SUB : (k + 1) * SUB]
                gsend[it, k, SUB : SUB + 2] = stats
            to_peers("row", send_sums)
            rs[it, r] = gsend[it, r]

        if it == 0:
            loads[3].wait()
            loads[4].wait()
            rows, cols = rows_ref[...], cols_ref[...]
            place = lax.broadcasted_iota(I32, (NB, TILE), 1)
            table = jnp.zeros((NB, TILE), I32)
            for at, col in enumerate(first_and_last(cols, rows) + first_and_last(rows, cols)):
                table = jnp.where(place == at, col, table)
            order_v[...] = table
            to_smem = pltpu.make_async_copy(order_v, order, order_sem)
            to_smem.start()
            loads[5].wait()
            for k in range(TILES):
                t_high, t_low = split2(tiles[k])
                tb[k, :, 0:TILE] = t_high
                tb[k, :, TILE : 2 * TILE] = t_low
            to_smem.wait()

        def put(b, row):
            rx[it, r, b : b + 1, :] = row

        products(order, 0, tb, yv, picked, put)
        if it == 0:

            @pl.when(late)
            def _():
                pl.semaphore_wait(barrier, len(near) + 2 * (G - 1))
                vouch()
                for to in range(EARLY):
                    pl.semaphore_signal(here_sem, inc=1, device_id={"col": to}, device_id_type=MESH)

        spread("row", rx.at[it, r], *sem(1))

        def sum_rows():
            wait_bytes(rs.at[it, pl.ds(0, G - 1), pl.ds(0, srows)], recv_sem.at[it, 0])
            sx[it, s, 0:srows] = jnp.sum(rs[it, :, 0:srows], axis=0)
            spread("season", sx.at[it, s, pl.ds(0, srows)], *sem(2))

        def sum_seasons():
            wait_bytes(sx.at[it, pl.ds(0, G - 1), pl.ds(0, srows)], recv_sem.at[it, 2])
            return jnp.sum(sx[it, :, 0:srows], axis=0)

        if it == 0:
            pl.semaphore_wait(far_sem, len(at_two))
            pl.when(early)(sum_rows)
            for k in range(TILES):
                t_high, t_low = split2(tiles[k].T)
                tf[k, :, 0:TILE] = t_high
                tf[k, :, TILE : 2 * TILE] = t_low
            for load in loads[6:]:
                load.wait()
        else:
            sum_rows()
        wait_bytes(rx.at[it, pl.ds(0, G - 1)], recv_sem.at[it, 1])
        transposed = jnp.sum(rx[it], axis=0)
        if it == 0:
            primal_step, dual_step = jnp.full((1, 1), STEP_SCALE, F32), jnp.full((1, 1), STEP_SCALE, F32)
        else:
            total = sum_seasons()
            dual_sq = jnp.sum(total[SUB : SUB + 1], axis=1, keepdims=True)
            primal_sq = jnp.sum(total[SUB + 1 : SUB + 2], axis=1, keepdims=True) * (1.0 / G)
            square = jnp.sqrt(primal_sq + EPSILON) * lax.rsqrt(dual_sq + EPSILON)
            if balance is not None:
                square = balance * square
            balance = jnp.sqrt(square)
            primal_step, dual_step = STEP_SCALE * lax.rsqrt(square), STEP_SCALE * balance
            if it == 1:
                @pl.when(late)
                def _():
                    wait_bytes(z_in, pair_sem.at[0])
                    zv[...] = z_in[...]

            z_old = zv[...]
            z_new = jnp.maximum(z_old - primal_step * (costz[...] - total[0:SUB]), 0.0)
            zv[...] = z_new
            ez[it, r, 0:SUB] = 2.0 * z_new - z_old
            spread("row", ez.at[it, r, pl.ds(0, SUB)], *sem(3))
            z_change = jnp.sum((z_new - z_old) ** 2, axis=0, keepdims=True)
        if last:
            z_out[c, r] = z_new
            send_z(0, "col", z_out.at[c, r, TWO_STEPS])

        x_old = xv[...]
        x_new = jnp.clip(x_old - primal_step * (costx_ref[...] - transposed), 0.0, upper_ref[...])
        xv[...] = x_new
        tr[...] = 2.0 * x_new - x_old

        def put(b, row):
            fw[b : b + 1, :] = row

        products(order, 4, tf, tr, picked, put)
        if last:
            x_out[...] = x_new
            for to_c in [c] + others("col"):
                for to_r in [r] + others("row"):
                    if to_c is not c or to_r is not r:
                        pltpu.make_async_remote_copy(
                            src_ref=z_out.at[c, r, STRAIGHT], dst_ref=z_out.at[c, r, STRAIGHT],
                            send_sem=zs_sem.at[2], recv_sem=zr_sem.at[2],
                            device_id={"row": to_r, "col": to_c}, device_id_type=MESH,
                        ).start()
        x_change = jnp.sum((x_new - x_old) ** 2, axis=0, keepdims=True)

        if it == 0:

            @pl.when(early)
            def _():
                total = sum_seasons()
                z_old = jnp.concatenate([zv[...]] + [z_more[k] for k in range(SHARE - 1)], axis=0)
                cost = jnp.concatenate([costz[...]] + [costz_more[k] for k in range(SHARE - 1)], axis=0)
                z_new = jnp.maximum(z_old - STEP_SCALE * (cost - total), 0.0)
                zv[...] = z_new[0:SUB]
                for k in range(1, SHARE):
                    z_more[k - 1] = z_new[k * SUB : (k + 1) * SUB]
                ez[0, r] = 2.0 * z_new - z_old
                spread("row", ez.at[0, r], *sem(3))
                cx[0, c, NB : NB + 1] = x_change + jnp.sum((z_new - z_old) ** 2, axis=0, keepdims=True)
                pl.semaphore_wait(here_sem, G - EARLY)
                for k in range(1, SHARE):
                    z_to(k).start()
                wait_bytes(ez.at[0, pl.ds(0, G - 1)], recv_sem.at[0, 3])
                parts = [
                    linked(k, ez[0, :, k * SUB : (k + 1) * SUB].reshape(CH, TILE)) for k in range(SHARE)
                ]
                for each in zip(*parts):
                    n = each[0][0]
                    cx[0, c, n : n + 1] = fw[n : n + 1, :] + sum(row for _, row in each)

            @pl.when(late)
            def _():
                cx[0, c, 0:NB] = fw[...]
                cx[0, c, NB : NB + 1] = x_change

        else:
            if not last:
                cx[it, c, NB : NB + 1] = x_change + z_change
            wait_bytes(ez.at[it, pl.ds(0, G - 1), pl.ds(0, SUB)], recv_sem.at[it, 3])
            for n, one in linked(0, ez[it, :, 0:SUB].reshape(CH, TILE)):
                cx[it, c, n : n + 1] = fw[n : n + 1, :] + one
        spread("col", cx.at[it, c, pl.ds(0, crows)], *sem(4))
        if last:
            wait_bytes(z_out.at[pl.ds(0, G - 1), 0, TWO_STEPS], zr_sem.at[0])
            send_z(1, "row", z_out.at[:, r, TWO_STEPS])
        wait_bytes(cx.at[it, pl.ds(0, G - 1), pl.ds(0, crows)], recv_sem.at[it, 4])
        image = jnp.sum(cx[it, :, 0:crows], axis=0)

        y_old = yv[...]
        y_new = jnp.maximum(y_old + dual_step * (rhs_ref[...] - image[0:NB]), 0.0)
        yv[...] = y_new
        if last:
            y_out[...] = y_new
        else:
            stats = jnp.concatenate(
                [jnp.sum((y_new - y_old) ** 2, axis=0, keepdims=True), image[NB : NB + 1]], axis=0
            )

    wait_bytes(z_out.at[pl.ds(0, G - 1), :, TWO_STEPS], zr_sem.at[1])
    wait_bytes(z_out.at[pl.ds(0, G - 1), 0, TWO_STEPS], zs_sem.at[0])
    wait_bytes(z_out.at[pl.ds(0, G - 1), :, TWO_STEPS], zs_sem.at[1])
    for sem in (zr_sem.at[2], zs_sem.at[2]):
        wait_bytes(rows_in.at[pl.ds(0, 3 * (G * G - 1))], sem)
    for it in range(ITERS):
        srows = SHARE * SUB if it == 0 else SUB + 2
        erows = SHARE * SUB if it == 0 else SUB
        crows = NB if it + 1 == ITERS else NB + 1

        def sent():
            wait_bytes(gsend.at[it, pl.ds(0, G - 1), pl.ds(0, srows)], send_sem.at[it, 0])
            wait_bytes(sx.at[it, pl.ds(0, G - 1), pl.ds(0, srows)], send_sem.at[it, 2])
            wait_bytes(ez.at[it, pl.ds(0, G - 1), pl.ds(0, erows)], send_sem.at[it, 3])
            if it == 0:
                for k in range(1, SHARE):
                    z_to(k).wait_send()

        if it == 0:
            pl.when(early)(sent)
        else:
            sent()
        wait_bytes(rx.at[it, pl.ds(0, G - 1)], send_sem.at[it, 1])
        wait_bytes(cx.at[it, pl.ds(0, G - 1), pl.ds(0, crows)], send_sem.at[it, 4])


def place(x_ref, z_ref, y_ref, x_out, z_out, y_out, sem):
    copies = [
        pltpu.make_async_copy(here, there, sem.at[k])
        for k, (here, there) in enumerate([(z_ref, z_out), (x_ref, x_out), (y_ref, y_out)])
    ]
    for copy in copies:
        copy.start()
    for copy in copies:
        copy.wait()


def local(
    tiles, tile_rows, tile_cols, rhs, coupling, asset, cost_x, upper, cost_z, x_init, z_init, y_init
):
    block = lambda a: a.reshape(NB, TILE)
    inside = pl.BlockSpec(memory_space=pltpu.VMEM)
    in_hbm = lambda a: pltpu.with_memory_space_constraint(a, pltpu.HBM)
    in_vmem = lambda a: pltpu.with_memory_space_constraint(a, pltpu.VMEM)
    operands = (
        tiles.reshape(TILES, TILE, TILE),
        tile_rows.reshape(1, TILES),
        tile_cols.reshape(1, TILES),
        block(rhs),
        block(coupling),
        block(asset),
        block(cost_x),
        block(upper),
        cost_z.reshape(G * CH, TILE),
        block(x_init),
        z_init.reshape(G * CH, TILE),
        block(y_init),
    )
    x, z, y = pl.pallas_call(
        kernel,
        out_shape=(
            pltpu.VMEM((NB, TILE), F32), pltpu.VMEM((G, G, SUB, TILE), F32), pltpu.VMEM((NB, TILE), F32),
        ),
        in_specs=[pl.BlockSpec(memory_space=pltpu.HBM)] * 12,
        out_specs=(inside, inside, inside),
        scratch_shapes=[
            pltpu.VMEM((TILES, TILE, TILE), F32),
            pltpu.VMEM((1, TILES), I32),
            pltpu.VMEM((1, TILES), I32),
            pltpu.VMEM((NB, TILE), F32),
            pltpu.VMEM((NB, TILE), F32),
            pltpu.VMEM((NB, TILE), I32),
            pltpu.VMEM((NB, TILE), F32),
            pltpu.VMEM((NB, TILE), F32),
            pltpu.VMEM((SUB, TILE), F32),
            pltpu.VMEM((NB, TILE), F32),
            pltpu.VMEM((SUB, TILE), F32),
            pltpu.VMEM((NB, TILE), F32),
            pltpu.VMEM((SHARE - 1, SUB, TILE), F32),
            pltpu.VMEM((SHARE - 1, SUB, TILE), F32),
            pltpu.VMEM((SUB, TILE), F32),
            pltpu.VMEM((TILES, TILE, 2 * TILE), BF16),
            pltpu.VMEM((TILES, TILE, 2 * TILE), BF16),
            pltpu.VMEM((NB, TILE), F32),
            pltpu.VMEM((NB, TILE), F32),
            pltpu.VMEM((NB, 2 * TILE), F32),
            pltpu.VMEM((NB, TILE), I32),
            pltpu.SMEM((NB, TILE), I32),
            pltpu.VMEM((SHARE, CH, NB * TILE), F32),
            pltpu.VMEM((SHARE, CH, NB * TILE), BF16),
            pltpu.VMEM((2 * TILE, NB * TILE), BF16),
            pltpu.VMEM((SHARE, 2 * CH, NB * TILE), BF16),
            pltpu.VMEM((ITERS, G, SHARE * SUB, TILE), F32),
            pltpu.VMEM((ITERS, G, SHARE * SUB, TILE), F32),
            pltpu.VMEM((ITERS, G, NB, TILE), F32),
            pltpu.VMEM((ITERS, G, SHARE * SUB, TILE), F32),
            pltpu.VMEM((ITERS, G, SHARE * SUB, TILE), F32),
            pltpu.VMEM((ITERS, G, NB + 1, TILE), F32),
            pltpu.VMEM((3 * G * G, TILE), F32),
            pltpu.SemaphoreType.DMA((12 + 2 * (SHARE - 1),)),
            pltpu.SemaphoreType.DMA,
            pltpu.SemaphoreType.DMA((ITERS, 5)),
            pltpu.SemaphoreType.DMA((ITERS, 5)),
            pltpu.SemaphoreType.DMA((3,)),
            pltpu.SemaphoreType.DMA((3,)),
            pltpu.SemaphoreType.DMA((SHARE,)),
            pltpu.SemaphoreType.REGULAR,
            pltpu.SemaphoreType.REGULAR,
        ],
        compiler_params=pltpu.CompilerParams(
            collective_id=0, has_side_effects=True, vmem_limit_bytes=VMEM_LIMIT
        ),
    )(*map(in_hbm, operands))
    x, z, y = pl.pallas_call(
        place,
        out_shape=tuple(jax.ShapeDtypeStruct(a.shape, F32) for a in (x, z, y)),
        in_specs=[inside] * 3,
        out_specs=(pl.BlockSpec(memory_space=pl.ANY),) * 3,
        scratch_shapes=[pltpu.SemaphoreType.DMA((3,))],
    )(*map(in_vmem, (x, z, y)))
    return x.reshape(1, -1), z.reshape(-1), y.reshape(1, -1)


def solution(mesh):
    in_specs = (
        P("season", "row", "col", None, None, None),
        P("season", "row", "col", None),
        P("season", "row", "col", None),
        P("season", "row"),
        P("season", "row"),
        P("season", "row"),
        P("season", "col"),
        P("season", "col"),
        P(),
        P("season", "col"),
        P(),
        P("season", "row"),
    )
    out_specs = (P("season", "col"), P(), P("season", "row"))
    return jax.shard_map(local, mesh=mesh, in_specs=in_specs, out_specs=out_specs, check_vma=False)
```

```python
import functools

import jax
import jax.numpy as jnp
from jax import lax
from jax.experimental import pallas as pl
from jax.experimental.pallas import tpu as pltpu
from jax.sharding import PartitionSpec as P

ITERS = 3
STEP_SCALE = 0.35
EPSILON = 1e-06
VMEM_LIMIT = 32 * 1024 * 1024

MESH = pl.DeviceIdType.MESH
F32, BF16, I32 = jnp.float32, jnp.bfloat16, jnp.int32
G = 8
NB = 16
TILE = 128
TILES = 32
CH = 64
SUB = CH // G
EARLY = 2
SHARE = G // EARLY
STRAIGHT, TWO_STEPS = pl.ds(0, 3), pl.ds(3, SUB - 3)


NEAR = {"season": 8, "row": 4, "col": 2}
FAR_FIRST = {
    "season": [(0, 4), (0, 3), (0, 5), (0, 2), (0, 6), (0, 1), (0, 7)],
    "row": [(1, 2), (0, 2), (1, 1), (1, 3), (0, 1), (0, 3), (1, 0)],
    "col": [(2, 0), (2, 1), (1, 0), (3, 0), (1, 1), (3, 1), (0, 1)],
}


def others(axis):
    me, n = lax.axis_index(axis), NEAR[axis]
    i, j = me // n, lax.rem(me, n)
    return [lax.rem(i + a, G // n) * n + lax.rem(j + b, n) for a, b in FAR_FIRST[axis]]


def to_peers(axis, copy):
    for to in others(axis):
        copy(to, {axis: to})


def wait_bytes(ref, sem):
    pltpu.make_async_copy(ref, ref, sem).wait()


def split2(v):
    high = v.astype(BF16)
    return high, (v - high.astype(F32)).astype(BF16)


def first_and_last(keys, other):
    k = lax.broadcasted_iota(I32, (NB, TILES), 1)
    hit = keys == lax.broadcasted_iota(I32, (NB, TILES), 0)
    one = jnp.min(jnp.where(hit, k, TILES - 1), axis=1, keepdims=True)
    two = jnp.max(jnp.where(hit, k, 0), axis=1, keepdims=True)
    pick = lambda t: jnp.sum(jnp.where(k == t, other, 0), axis=1, keepdims=True)
    return one, two, pick(one), pick(two)


def products(order, column, tiles_ref, values_ref, picked, out):
    for b in range(NB):
        picked[b : b + 1, 0:TILE] = values_ref[pl.ds(order[b, column + 2], 1), :]
        picked[b : b + 1, TILE : 2 * TILE] = values_ref[pl.ds(order[b, column + 3], 1), :]
    high, low = split2(picked[...])
    left = jnp.concatenate([high, low], axis=0)
    for b in range(NB):
        right = jnp.concatenate(
            [tiles_ref[order[b, column]], tiles_ref[order[b, column + 1]]], axis=0
        )
        res = jnp.dot(left, right, preferred_element_type=F32)
        row = res[b : b + 1, :] + res[NB + b : NB + b + 1, :]
        out(b, row[:, 0:TILE] + row[:, TILE : 2 * TILE])


def kernel(
    tiles_hbm, rows_hbm, cols_hbm, rhs_hbm, coup_hbm, asset_hbm, costx_hbm, upper_hbm, costz_hbm, x0_hbm, z0_hbm, y0_hbm,
    x_out, z_out, y_out,
    tiles, rows_ref, cols_ref, rhs_ref, coup_ref, asset_ref, costx_ref, upper_ref, costz, xv, zv, yv,
    costz_more, z_more, z_in, tb, tf, tr, fw, picked, order_v, order, mask, hot_hi, hot_lo, left,
    gsend, rs, rx, sx, ez, cx, rows_in,
    load_sem, order_sem, send_sem, recv_sem, zs_sem, zr_sem, pair_sem, here_sem, far_sem, col_sem,
):
    s, r, c = (lax.axis_index(a) for a in ("season", "row", "col"))
    barrier = pltpu.get_barrier_semaphore()
    early, late = c < EARLY, c >= EARLY
    at_two = [lax.rem(s + k, G) for k in (2, G - 2)]
    near = at_two + [lax.rem(s + k, G) for k in (1, G - 1)]
    for axis, peers in (("season", near), ("row", others("row"))):
        for to in peers:
            pl.semaphore_signal(barrier, inc=1, device_id={axis: to}, device_id_type=MESH)
    for to in others("col"):
        near_col = jnp.logical_and(to >= EARLY, jnp.abs(to // 2 - c // 2) <= 1)

        @pl.when(jnp.logical_or(early, near_col))
        def _():
            pl.semaphore_signal(barrier, inc=1, device_id={"col": to}, device_id_type=MESH)

    mine = pl.ds(pl.multiple_of(c * CH + r * SUB, SUB), SUB)
    more = [pl.ds(pl.multiple_of(lax.rem(c + EARLY * k, G) * CH + r * SUB, SUB), SUB) for k in range(1, SHARE)]
    loads = [
        pltpu.make_async_copy(there, here, load_sem.at[k])
        for k, (there, here) in enumerate([
            (asset_hbm, asset_ref), (coup_hbm, coup_ref), (y0_hbm, yv), (rows_hbm, rows_ref), (cols_hbm, cols_ref),
            (tiles_hbm, tiles), (costz_hbm.at[mine], costz), (z0_hbm.at[mine], zv), (x0_hbm, xv),
            (costx_hbm, costx_ref), (upper_hbm, upper_ref), (rhs_hbm, rhs_ref),
        ] + [(costz_hbm.at[at], costz_more.at[k]) for k, at in enumerate(more)]
          + [(z0_hbm.at[at], z_more.at[k]) for k, at in enumerate(more)])
    ]
    for load in loads:
        load.start()

    loads[0].wait()
    asset = asset_ref[...]
    low, high = asset & (TILE - 1), (asset >> 7) - c * CH
    for n in range(NB):
        at = slice(n * TILE, (n + 1) * TILE)
        hit = lax.broadcasted_iota(I32, (TILE, TILE), 0) == low[n : n + 1, :]
        one = jnp.where(hit, 1.0, 0.0).astype(BF16)
        hot_lo[0:TILE, at] = one
        hot_lo[TILE : 2 * TILE, at] = one
        hit = lax.broadcasted_iota(I32, (CH, TILE), 0) == high[n : n + 1, :]
        one = jnp.where(hit, 1.0, 0.0)
        mask[0, :, at] = one
        hot_hi[0, :, at] = one.astype(BF16)

    @pl.when(early)
    def _():
        for k in range(1, SHARE):
            for n in range(NB):
                at = slice(n * TILE, (n + 1) * TILE)
                hit = lax.broadcasted_iota(I32, (CH, TILE), 0) == high[n : n + 1, :] - k * EARLY * CH
                one = jnp.where(hit, 1.0, 0.0)
                mask[k, :, at] = one
                hot_hi[k, :, at] = one.astype(BF16)

    loads[1].wait()
    loads[2].wait()
    coup = coup_ref[...]

    def spread(axis, blocks, send, recv):
        def start(to, device):
            pltpu.make_async_remote_copy(
                src_ref=blocks, dst_ref=blocks, send_sem=send, recv_sem=recv, device_id=device, device_id_type=MESH
            ).start()

        to_peers(axis, start)

    def z_to(k):
        return pltpu.make_async_remote_copy(
            src_ref=z_more.at[k - 1], dst_ref=z_in, send_sem=pair_sem.at[k], recv_sem=pair_sem.at[0],
            device_id={"col": c + k * EARLY}, device_id_type=MESH,
        )

    def send_z(k, axis, blocks):
        spread(axis, blocks, zs_sem.at[k], zr_sem.at[k])

    def vouch():
        for to in at_two:
            pl.semaphore_signal(far_sem, inc=1, device_id={"season": to}, device_id_type=MESH)

    def investment(k):
        v_high, v_low = split2(coup * yv[...])
        for n in range(NB):
            at = slice(n * TILE, (n + 1) * TILE)
            hot = hot_hi[k, :, at]
            left[k, 0:CH, at] = hot * v_high[n : n + 1, :]
            left[k, CH : 2 * CH, at] = hot * v_low[n : n + 1, :]
        cap = lax.dot_general(
            left[k], hot_lo[0:TILE, :], (((1,), (1,)), ((), ())), preferred_element_type=F32
        )
        return cap[0:CH] + cap[CH : 2 * CH]

    def linked(k, values):
        e_high, e_low = split2(values)
        gathered = jnp.dot(
            jnp.concatenate([e_high, e_low], axis=1), hot_lo[...], preferred_element_type=F32
        )
        for n in range(NB):
            at = slice(n * TILE, (n + 1) * TILE)
            yield n, coup[n : n + 1, :] * jnp.sum(gathered[:, at] * mask[k, :, at], axis=0, keepdims=True)

    balance = None
    stats = None
    for it in range(ITERS):
        last = it + 1 == ITERS
        srows = SHARE * SUB if it == 0 else SUB + 2
        crows = NB if last else NB + 1
        sem = lambda phase: (send_sem.at[it, phase], recv_sem.at[it, phase])

        def send_sums(to, device):
            pltpu.make_async_remote_copy(
                src_ref=gsend.at[it, to, pl.ds(0, srows)], dst_ref=rs.at[it, r, pl.ds(0, srows)],
                send_sem=send_sem.at[it, 0], recv_sem=recv_sem.at[it, 0], device_id=device, device_id_type=MESH,
            ).start()

        if it == 0:

            @pl.when(early)
            def _():
                for half in range(SHARE):
                    cap = investment(half)
                    for k in range(G):
                        gsend[0, k, half * SUB : (half + 1) * SUB] = cap[k * SUB : (k + 1) * SUB]
                pl.semaphore_wait(barrier, len(near) + G - 1 + EARLY - 1)
                vouch()
                to_peers("row", send_sums)
                rs[0, r] = gsend[0, r]

        else:
            cap = investment(0)
            for k in range(G):
                gsend[it, k, 0:SUB] = cap[k * SUB : (k + 1) * SUB]
                gsend[it, k, SUB : SUB + 2] = stats
            to_peers("row", send_sums)
            rs[it, r] = gsend[it, r]

        if it == 0:
            loads[3].wait()
            loads[4].wait()
            rows, cols = rows_ref[...], cols_ref[...]
            place = lax.broadcasted_iota(I32, (NB, TILE), 1)
            table = jnp.zeros((NB, TILE), I32)
            for at, col in enumerate(first_and_last(cols, rows) + first_and_last(rows, cols)):
                table = jnp.where(place == at, col, table)
            order_v[...] = table
            to_smem = pltpu.make_async_copy(order_v, order, order_sem)
            to_smem.start()
            loads[5].wait()
            for k in range(TILES):
                t_high, t_low = split2(tiles[k])
                tb[k, :, 0:TILE] = t_high
                tb[k, :, TILE : 2 * TILE] = t_low
            to_smem.wait()

        def put(b, row):
            rx[it, r, b : b + 1, :] = row

        products(order, 0, tb, yv, picked, put)
        if it == 0:

            @pl.when(late)
            def _():
                middle = c // 2 == 2
                pl.semaphore_wait(barrier, len(near) + G - 1 + jnp.where(middle, G - 1, G - 3))
                vouch()

                @pl.when(middle)
                def _():
                    for to in (c - 2, c + 2):
                        pl.semaphore_signal(col_sem, inc=1, device_id={"col": to}, device_id_type=MESH)

                for to in range(EARLY):
                    pl.semaphore_signal(here_sem, inc=1, device_id={"col": to}, device_id_type=MESH)

        spread("row", rx.at[it, r], *sem(1))

        def sum_rows():
            wait_bytes(rs.at[it, pl.ds(0, G - 1), pl.ds(0, srows)], recv_sem.at[it, 0])
            sx[it, s, 0:srows] = jnp.sum(rs[it, :, 0:srows], axis=0)
            spread("season", sx.at[it, s, pl.ds(0, srows)], *sem(2))

        def sum_seasons():
            wait_bytes(sx.at[it, pl.ds(0, G - 1), pl.ds(0, srows)], recv_sem.at[it, 2])
            return jnp.sum(sx[it, :, 0:srows], axis=0)

        if it == 0:
            pl.semaphore_wait(far_sem, len(at_two))
            pl.when(early)(sum_rows)
            for k in range(TILES):
                t_high, t_low = split2(tiles[k].T)
                tf[k, :, 0:TILE] = t_high
                tf[k, :, TILE : 2 * TILE] = t_low
            for load in loads[6:]:
                load.wait()
        else:
            sum_rows()
        wait_bytes(rx.at[it, pl.ds(0, G - 1)], recv_sem.at[it, 1])
        transposed = jnp.sum(rx[it], axis=0)
        if it == 0:
            primal_step, dual_step = jnp.full((1, 1), STEP_SCALE, F32), jnp.full((1, 1), STEP_SCALE, F32)
        else:
            total = sum_seasons()
            dual_sq = jnp.sum(total[SUB : SUB + 1], axis=1, keepdims=True)
            primal_sq = jnp.sum(total[SUB + 1 : SUB + 2], axis=1, keepdims=True) * (1.0 / G)
            square = jnp.sqrt(primal_sq + EPSILON) * lax.rsqrt(dual_sq + EPSILON)
            if balance is not None:
                square = balance * square
            balance = jnp.sqrt(square)
            primal_step, dual_step = STEP_SCALE * lax.rsqrt(square), STEP_SCALE * balance
            if it == 1:
                @pl.when(late)
                def _():
                    wait_bytes(z_in, pair_sem.at[0])
                    zv[...] = z_in[...]

            z_old = zv[...]
            z_new = jnp.maximum(z_old - primal_step * (costz[...] - total[0:SUB]), 0.0)
            zv[...] = z_new
            ez[it, r, 0:SUB] = 2.0 * z_new - z_old
            spread("row", ez.at[it, r, pl.ds(0, SUB)], *sem(3))
            z_change = jnp.sum((z_new - z_old) ** 2, axis=0, keepdims=True)
        if last:
            z_out[c, r] = z_new
            send_z(0, "col", z_out.at[c, r, TWO_STEPS])

        x_old = xv[...]
        x_new = jnp.clip(x_old - primal_step * (costx_ref[...] - transposed), 0.0, upper_ref[...])
        xv[...] = x_new
        tr[...] = 2.0 * x_new - x_old

        def put(b, row):
            fw[b : b + 1, :] = row

        products(order, 4, tf, tr, picked, put)
        if last:
            x_out[...] = x_new
            for to_c in [c] + others("col"):
                for to_r in [r] + others("row"):
                    if to_c is not c or to_r is not r:
                        pltpu.make_async_remote_copy(
                            src_ref=z_out.at[c, r, STRAIGHT], dst_ref=z_out.at[c, r, STRAIGHT],
                            send_sem=zs_sem.at[2], recv_sem=zr_sem.at[2],
                            device_id={"row": to_r, "col": to_c}, device_id_type=MESH,
                        ).start()
        x_change = jnp.sum((x_new - x_old) ** 2, axis=0, keepdims=True)

        if it == 0:

            @pl.when(early)
            def _():
                total = sum_seasons()
                z_old = jnp.concatenate([zv[...]] + [z_more[k] for k in range(SHARE - 1)], axis=0)
                cost = jnp.concatenate([costz[...]] + [costz_more[k] for k in range(SHARE - 1)], axis=0)
                z_new = jnp.maximum(z_old - STEP_SCALE * (cost - total), 0.0)
                zv[...] = z_new[0:SUB]
                for k in range(1, SHARE):
                    z_more[k - 1] = z_new[k * SUB : (k + 1) * SUB]
                ez[0, r] = 2.0 * z_new - z_old
                spread("row", ez.at[0, r], *sem(3))
                cx[0, c, NB : NB + 1] = x_change + jnp.sum((z_new - z_old) ** 2, axis=0, keepdims=True)
                pl.semaphore_wait(here_sem, G - EARLY)
                for k in range(1, SHARE):
                    z_to(k).start()
                wait_bytes(ez.at[0, pl.ds(0, G - 1)], recv_sem.at[0, 3])
                parts = [
                    linked(k, ez[0, :, k * SUB : (k + 1) * SUB].reshape(CH, TILE)) for k in range(SHARE)
                ]
                for each in zip(*parts):
                    n = each[0][0]
                    cx[0, c, n : n + 1] = fw[n : n + 1, :] + sum(row for _, row in each)

            @pl.when(late)
            def _():
                cx[0, c, 0:NB] = fw[...]

                @pl.when(c // 2 != 2)
                def _():
                    pl.semaphore_wait(col_sem, 1)

                cx[0, c, NB : NB + 1] = x_change

        else:
            if not last:
                cx[it, c, NB : NB + 1] = x_change + z_change
            wait_bytes(ez.at[it, pl.ds(0, G - 1), pl.ds(0, SUB)], recv_sem.at[it, 3])
            for n, one in linked(0, ez[it, :, 0:SUB].reshape(CH, TILE)):
                cx[it, c, n : n + 1] = fw[n : n + 1, :] + one
        spread("col", cx.at[it, c, pl.ds(0, crows)], *sem(4))
        if last:
            wait_bytes(z_out.at[pl.ds(0, G - 1), 0, TWO_STEPS], zr_sem.at[0])
            send_z(1, "row", z_out.at[:, r, TWO_STEPS])
        wait_bytes(cx.at[it, pl.ds(0, G - 1), pl.ds(0, crows)], recv_sem.at[it, 4])
        image = jnp.sum(cx[it, :, 0:crows], axis=0)

        y_old = yv[...]
        y_new = jnp.maximum(y_old + dual_step * (rhs_ref[...] - image[0:NB]), 0.0)
        yv[...] = y_new
        if last:
            y_out[...] = y_new
        else:
            stats = jnp.concatenate(
                [jnp.sum((y_new - y_old) ** 2, axis=0, keepdims=True), image[NB : NB + 1]], axis=0
            )

    wait_bytes(z_out.at[pl.ds(0, G - 1), :, TWO_STEPS], zr_sem.at[1])
    wait_bytes(z_out.at[pl.ds(0, G - 1), 0, TWO_STEPS], zs_sem.at[0])
    wait_bytes(z_out.at[pl.ds(0, G - 1), :, TWO_STEPS], zs_sem.at[1])
    for sem in (zr_sem.at[2], zs_sem.at[2]):
        wait_bytes(rows_in.at[pl.ds(0, 3 * (G * G - 1))], sem)
    for it in range(ITERS):
        srows = SHARE * SUB if it == 0 else SUB + 2
        erows = SHARE * SUB if it == 0 else SUB
        crows = NB if it + 1 == ITERS else NB + 1

        def sent():
            wait_bytes(gsend.at[it, pl.ds(0, G - 1), pl.ds(0, srows)], send_sem.at[it, 0])
            wait_bytes(sx.at[it, pl.ds(0, G - 1), pl.ds(0, srows)], send_sem.at[it, 2])
            wait_bytes(ez.at[it, pl.ds(0, G - 1), pl.ds(0, erows)], send_sem.at[it, 3])
            if it == 0:
                for k in range(1, SHARE):
                    z_to(k).wait_send()

        if it == 0:
            pl.when(early)(sent)
        else:
            sent()
        wait_bytes(rx.at[it, pl.ds(0, G - 1)], send_sem.at[it, 1])
        wait_bytes(cx.at[it, pl.ds(0, G - 1), pl.ds(0, crows)], send_sem.at[it, 4])


def place(x_ref, z_ref, y_ref, x_out, z_out, y_out, sem):
    copies = [
        pltpu.make_async_copy(here, there, sem.at[k])
        for k, (here, there) in enumerate([(z_ref, z_out), (x_ref, x_out), (y_ref, y_out)])
    ]
    for copy in copies:
        copy.start()
    for copy in copies:
        copy.wait()


def local(
    tiles, tile_rows, tile_cols, rhs, coupling, asset, cost_x, upper, cost_z, x_init, z_init, y_init
):
    block = lambda a: a.reshape(NB, TILE)
    inside = pl.BlockSpec(memory_space=pltpu.VMEM)
    in_hbm = lambda a: pltpu.with_memory_space_constraint(a, pltpu.HBM)
    in_vmem = lambda a: pltpu.with_memory_space_constraint(a, pltpu.VMEM)
    operands = (
        tiles.reshape(TILES, TILE, TILE),
        tile_rows.reshape(1, TILES),
        tile_cols.reshape(1, TILES),
        block(rhs),
        block(coupling),
        block(asset),
        block(cost_x),
        block(upper),
        cost_z.reshape(G * CH, TILE),
        block(x_init),
        z_init.reshape(G * CH, TILE),
        block(y_init),
    )
    x, z, y = pl.pallas_call(
        kernel,
        out_shape=(
            pltpu.VMEM((NB, TILE), F32), pltpu.VMEM((G, G, SUB, TILE), F32), pltpu.VMEM((NB, TILE), F32),
        ),
        in_specs=[pl.BlockSpec(memory_space=pltpu.HBM)] * 12,
        out_specs=(inside, inside, inside),
        scratch_shapes=[
            pltpu.VMEM((TILES, TILE, TILE), F32),
            pltpu.VMEM((1, TILES), I32),
            pltpu.VMEM((1, TILES), I32),
            pltpu.VMEM((NB, TILE), F32),
            pltpu.VMEM((NB, TILE), F32),
            pltpu.VMEM((NB, TILE), I32),
            pltpu.VMEM((NB, TILE), F32),
            pltpu.VMEM((NB, TILE), F32),
            pltpu.VMEM((SUB, TILE), F32),
            pltpu.VMEM((NB, TILE), F32),
            pltpu.VMEM((SUB, TILE), F32),
            pltpu.VMEM((NB, TILE), F32),
            pltpu.VMEM((SHARE - 1, SUB, TILE), F32),
            pltpu.VMEM((SHARE - 1, SUB, TILE), F32),
            pltpu.VMEM((SUB, TILE), F32),
            pltpu.VMEM((TILES, TILE, 2 * TILE), BF16),
            pltpu.VMEM((TILES, TILE, 2 * TILE), BF16),
            pltpu.VMEM((NB, TILE), F32),
            pltpu.VMEM((NB, TILE), F32),
            pltpu.VMEM((NB, 2 * TILE), F32),
            pltpu.VMEM((NB, TILE), I32),
            pltpu.SMEM((NB, TILE), I32),
            pltpu.VMEM((SHARE, CH, NB * TILE), F32),
            pltpu.VMEM((SHARE, CH, NB * TILE), BF16),
            pltpu.VMEM((2 * TILE, NB * TILE), BF16),
            pltpu.VMEM((SHARE, 2 * CH, NB * TILE), BF16),
            pltpu.VMEM((ITERS, G, SHARE * SUB, TILE), F32),
            pltpu.VMEM((ITERS, G, SHARE * SUB, TILE), F32),
            pltpu.VMEM((ITERS, G, NB, TILE), F32),
            pltpu.VMEM((ITERS, G, SHARE * SUB, TILE), F32),
            pltpu.VMEM((ITERS, G, SHARE * SUB, TILE), F32),
            pltpu.VMEM((ITERS, G, NB + 1, TILE), F32),
            pltpu.VMEM((3 * G * G, TILE), F32),
            pltpu.SemaphoreType.DMA((12 + 2 * (SHARE - 1),)),
            pltpu.SemaphoreType.DMA,
            pltpu.SemaphoreType.DMA((ITERS, 5)),
            pltpu.SemaphoreType.DMA((ITERS, 5)),
            pltpu.SemaphoreType.DMA((3,)),
            pltpu.SemaphoreType.DMA((3,)),
            pltpu.SemaphoreType.DMA((SHARE,)),
            pltpu.SemaphoreType.REGULAR,
            pltpu.SemaphoreType.REGULAR,
            pltpu.SemaphoreType.REGULAR,
        ],
        compiler_params=pltpu.CompilerParams(
            collective_id=0, has_side_effects=True, vmem_limit_bytes=VMEM_LIMIT
        ),
    )(*map(in_hbm, operands))
    x, z, y = pl.pallas_call(
        place,
        out_shape=tuple(jax.ShapeDtypeStruct(a.shape, F32) for a in (x, z, y)),
        in_specs=[inside] * 3,
        out_specs=(pl.BlockSpec(memory_space=pl.ANY),) * 3,
        scratch_shapes=[pltpu.SemaphoreType.DMA((3,))],
    )(*map(in_vmem, (x, z, y)))
    return x.reshape(1, -1), z.reshape(-1), y.reshape(1, -1)


def solution(mesh):
    in_specs = (
        P("season", "row", "col", None, None, None),
        P("season", "row", "col", None),
        P("season", "row", "col", None),
        P("season", "row"),
        P("season", "row"),
        P("season", "row"),
        P("season", "col"),
        P("season", "col"),
        P(),
        P("season", "col"),
        P(),
        P("season", "row"),
    )
    out_specs = (P("season", "col"), P(), P("season", "row"))
    return jax.shard_map(local, mesh=mesh, in_specs=in_specs, out_specs=out_specs, check_vma=False)
```
